32 devices in a mesh: stn: 2 (over y), tm: 8 (over z, core), cores: 2 (over x).
Axes of the slice: x: 2, y: 2, z: 4, core: 2. Of those that a mesh axis runs over, the one named last changes fastest.
Arguments:
- samples: bfloat16 [64, 2097152], P('stn', ('tm', 'cores')), may hold values from -6 to 6
- delays: int32 [64], P('stn'), may hold values from 0 to 32768, as said below
- valid: int32 [64], P('stn'), may hold values 0 or 1
- tone_chan: int32 [64, 64], P('stn'), may hold values from 0 to 16383
Outputs:
- visibility: float32 [16384, 8192], P(('stn', 'tm', 'cores'))
- phase_cal: float32 [64, 128], P('stn')
The draws below stay inside these ranges and needn't reach their ends.
Inputs may be any that keep to these rules, and one draw needn't show every extreme that they name: `delays`: each station's delay in samples; some station has a delay of exactly 32768.
All inputs are finite; a program needn't handle non-finite values. No bound on the sum of `valid` on one device may be relied on, other than what follows from the above.
Results may differ from the reference program's by a relative error of at most 0.007.
Values may be sent and summed in bfloat16 or wider, within the bound.
A program may use at most 128 MiB of HBM per device.

```python
import math
import jax
import jax.numpy as jnp
from jax import lax

S = 64
NCH = 16384
FA = 256
FB = 128
NTONE = 64
SPECTRA = 64
SAMPLES = 2097152
MAXD = 32768


def draw_delays(key, part):
    base = jax.random.fold_in(key, 17)
    key_one, key_two = jax.random.split(base)
    values = jax.random.randint(key_one, (S,), 0, MAXD + 1)
    chosen = jax.random.randint(key_two, (), 0, S)
    return jnp.where(jnp.arange(S) == chosen, MAXD, values).astype(jnp.int32)


def with_ends(values, rng, least, top_value):
    dims = values.shape
    index_at = [jax.random.randint(jax.random.fold_in(rng, axis), (), 0, dims[axis]) for axis in range(len(dims))]
    values = values.at[tuple(index_at)].set(least)
    longest = dims.index(max(dims))
    index_at[longest] = (index_at[longest] + 1) % dims[longest]
    return values.at[tuple(index_at)].set(top_value)


def shard_levels(key, dims, cuts, smallest, top_value):
    def one(dim, parts):
        heights = jax.random.uniform(jax.random.fold_in(jax.random.fold_in(key, 6), dim), (parts,), jnp.float32, smallest / len(cuts), top_value / len(cuts))
        return jnp.repeat(jnp.exp(heights), dims[dim] // parts).reshape((-1,) + (1,) * (len(dims) - dim - 1))

    level = one(*cuts[0])
    for cut in cuts[1:]:
        level = level * one(*cut)
    return level


def noise(stream_key, shape, width, limit, cuts=(), kind=jnp.bfloat16):
    array = jax.random.normal(stream_key, shape, jnp.float32) * width
    if len(cuts) > 0:
        array = shard_levels(stream_key, shape, cuts, -0.22, 0.18) * array
    return jnp.clip(array, min=-limit, max=limit).astype(kind)


def setup_inputs(seed: int = 0) -> dict:
    arg_keys = jax.random.split(jax.random.key(seed), 5)
    return {
        "samples": noise(arg_keys[0], (S, SAMPLES), 1.0, 6.0, ((0, 2), (1, 16))),
        "delays": draw_delays(jax.random.fold_in(arg_keys[4], 71), 0),
        "valid": with_ends((jax.random.randint(arg_keys[2], (S,), 0, 4) < 3).astype(jnp.int32), jax.random.fold_in(arg_keys[2], 1), 0, 1),
        "tone_chan": with_ends(jax.random.randint(arg_keys[3], (S, NTONE), 0, NCH), jax.random.fold_in(arg_keys[3], 1), 0, NCH - 1).astype(jnp.int32),
    }


def make_tables():
    outer_idx = jnp.arange(FA, dtype=jnp.int32)
    phases = outer_idx[:, None] * outer_idx[None, :] % FA
    angles = 2.0 * math.pi / FA * phases.astype(jnp.float32)
    section_one = jnp.stack([jnp.cos(angles), -jnp.sin(angles)]).astype(jnp.bfloat16)
    inner_idx = jnp.arange(FB, dtype=jnp.int32)
    spectrum_len = FA * FB
    twist_idx = outer_idx[:, None] * inner_idx[None, :] % spectrum_len
    twists = 2.0 * math.pi / spectrum_len * twist_idx.astype(jnp.float32)
    norm_scale = 1.0 / math.sqrt(spectrum_len)
    twist_cos = jnp.cos(twists) * norm_scale
    twist_sin = jnp.sin(twists) * norm_scale
    half_idx = jnp.arange(FB // 2, dtype=jnp.int32)
    last_idx = inner_idx[:, None] * half_idx[None, :] % FB
    thetas = 2.0 * math.pi / FB * last_idx.astype(jnp.float32)
    cosine = jnp.cos(thetas)
    sine_val = jnp.sin(thetas)
    section_two = jnp.stack([jnp.stack([cosine, -sine_val], axis=1), jnp.stack([sine_val, cosine], axis=1)]).astype(jnp.bfloat16)
    return (section_one, twist_cos, twist_sin, section_two)

def channelize(window, usable, tables):
    section_one, twist_cos, twist_sin, section_two = tables
    spec_count = window.shape[0] // (FA * FB)
    blocks = window.reshape(spec_count, FA, FB).astype(jnp.float32)
    section_out = jnp.einsum('xkn,bnm->bxkm', section_one.astype(jnp.float32), blocks)
    real_part = section_out[:, 0] * twist_cos + section_out[:, 1] * twist_sin
    imag_part = section_out[:, 1] * twist_cos - section_out[:, 0] * twist_sin
    twisted = jnp.stack([real_part, imag_part], axis=1).astype(jnp.bfloat16)
    twisted = lax.optimization_barrier(twisted).astype(jnp.float32)
    product = jnp.einsum('xnrq,bxkn->brqk', section_two.astype(jnp.float32), twisted)
    return (product.reshape(spec_count, 2, NCH) * usable).astype(jnp.bfloat16)

def reference(samples, delays, valid, tone_chan):
    tables = make_tables()
    stretch = samples.shape[1]

    def station(inputs):
        stream, shift_by, usable, tone_ids = inputs
        padded = jnp.concatenate([stream, jnp.zeros((MAXD,), stream.dtype)])
        window = lax.dynamic_slice_in_dim(padded, shift_by.astype(jnp.int32), stretch)
        spectra = channelize(window, usable.astype(jnp.float32), tables)
        widened = lax.optimization_barrier(spectra).astype(jnp.float32)
        totals = lax.optimization_barrier(jnp.sum(widened, axis=0))
        picked = jnp.take(totals, tone_ids, axis=1)
        return (spectra, picked.reshape(2 * NTONE))
    spectra, tone_picks = lax.map(station, (samples, delays, valid, tone_chan))
    norm_scale = 1.0 / math.sqrt(SPECTRA)
    phase_cal = tone_picks * norm_scale
    block_len = 128

    def gram_block(block_idx):
        piece_cut = lax.dynamic_slice_in_dim(spectra, block_idx * block_len, block_len, axis=3)
        widened = lax.optimization_barrier(piece_cut).astype(jnp.float32)
        rotated = jnp.stack([widened[:, :, 1], -widened[:, :, 0]], axis=2)
        stacked = jnp.stack([widened, rotated])
        gram_out = jnp.einsum('qitrc,jtrc->cqij', stacked, widened)
        return gram_out.reshape(block_len, 2 * S * S)
    visibility = lax.map(gram_block, jnp.arange(NCH // block_len, dtype=jnp.int32))
    visibility = visibility.reshape(NCH, 2 * S * S) * norm_scale
    return (visibility, phase_cal)
```

```python
import math

import jax
import jax.numpy as jnp
from jax import lax
from jax.experimental import pallas as pl
from jax.experimental.pallas import tpu as pltpu
from jax.sharding import PartitionSpec as P

S = 64
NCH = 16384
FA = 256
FB = 128
NTONE = 64
MAXD = 32768


def passed_along(block, axis, distance):
    devices = range(lax.axis_size(axis))
    route = [(i - distance, i) for i in devices if i - distance in devices]
    return lax.ppermute(block, axis, route)


def make_tables():
    outer_idx = jnp.arange(FA, dtype=jnp.int32)
    phases = outer_idx[:, None] * outer_idx[None, :] % FA
    angles = 2.0 * math.pi / FA * phases.astype(jnp.float32)
    section_one = jnp.stack([jnp.cos(angles), -jnp.sin(angles)]).astype(jnp.bfloat16)
    inner_idx = jnp.arange(FB, dtype=jnp.int32)
    spectrum_len = FA * FB
    twist_idx = outer_idx[:, None] * inner_idx[None, :] % spectrum_len
    twists = 2.0 * math.pi / spectrum_len * twist_idx.astype(jnp.float32)
    norm_scale = 1.0 / math.sqrt(spectrum_len)
    twist_cos = jnp.cos(twists) * norm_scale
    twist_sin = jnp.sin(twists) * norm_scale
    half_idx = jnp.arange(FB // 2, dtype=jnp.int32)
    last_idx = inner_idx[:, None] * half_idx[None, :] % FB
    thetas = 2.0 * math.pi / FB * last_idx.astype(jnp.float32)
    cosine = jnp.cos(thetas)
    sine_val = jnp.sin(thetas)
    section_two = jnp.stack(
        [jnp.stack([cosine, -sine_val], axis=1), jnp.stack([sine_val, cosine], axis=1)]
    ).astype(jnp.bfloat16)
    return (section_one, twist_cos, twist_sin, section_two)


def channelize(window, usable, tables):
    section_one, twist_cos, twist_sin, section_two = tables
    spec_count = window.shape[0] // (FA * FB)
    blocks = window.reshape(spec_count, FA, FB)
    section_out = jnp.einsum(
        "xkn,bnm->bxkm", section_one, blocks, preferred_element_type=jnp.float32
    )
    real_part = section_out[:, 0] * twist_cos + section_out[:, 1] * twist_sin
    imag_part = section_out[:, 1] * twist_cos - section_out[:, 0] * twist_sin
    twisted = jnp.stack([real_part, imag_part], axis=1).astype(jnp.bfloat16)
    product = jnp.einsum(
        "xnrq,bxkn->brqk", section_two, twisted, preferred_element_type=jnp.float32
    )
    return (product.reshape(spec_count, 2, NCH) * usable).astype(jnp.bfloat16)


def cross_power(matrix):
    gram = jnp.einsum("cta,ctb->cab", matrix, matrix, preferred_element_type=jnp.float32)
    real_re = gram[:, :S, :S]
    imag_im = gram[:, S:, S:]
    imag_re = gram[:, S:, :S]
    real_im = gram[:, :S, S:]
    channels = gram.shape[0]
    first = (real_re + imag_im).reshape(channels, S * S)
    second = (imag_re - real_im).reshape(channels, S * S)
    return jnp.concatenate([first, second], axis=1)


def shards(samples, delays, valid, tone_chan):
    tables = make_tables()
    stretch = samples.shape[1]
    spectrum_len = FA * FB
    trailing = passed_along(samples[:, :MAXD], ("tm", "cores"), -1)
    extended = jnp.concatenate([samples, trailing], axis=1)
    chan_ids = jnp.arange(NCH, dtype=jnp.int32)

    def station(inputs):
        stream, shift_by, usable, tone_ids = inputs
        window = lax.dynamic_slice_in_dim(stream, shift_by, stretch)
        spectra = channelize(window, usable.astype(jnp.float32), tables)
        totals = jnp.sum(spectra, axis=0, dtype=jnp.float32)
        selector = (chan_ids[:, None] == tone_ids[None, :]).astype(jnp.float32)
        picked = jnp.dot(
            totals, selector, precision=lax.Precision.HIGHEST, preferred_element_type=jnp.float32
        )
        return (spectra, picked.reshape(2 * NTONE))

    spectra, tone_picks = lax.map(station, (extended, delays, valid, tone_chan))
    spectra_all = stretch // spectrum_len * lax.axis_size("tm") * lax.axis_size("cores")
    norm_scale = 1.0 / math.sqrt(spectra_all)
    phase_cal = lax.psum(tone_picks, ("tm", "cores")) * norm_scale
    local_stn = spectra.shape[0]
    spec_here = spectra.shape[1]
    n_stn = lax.axis_size("stn")
    n_tm = lax.axis_size("tm")
    received = lax.all_to_all(spectra[None], ("stn", "tm"), split_axis=4, concat_axis=0, tiled=True)
    block_in = received.shape[4]
    arranged = received.reshape(n_stn, n_tm, local_stn, spec_here, 2, block_in)
    turned = jnp.transpose(arranged, (0, 2, 1, 3, 4, 5)).reshape(
        n_stn * local_stn, n_tm * spec_here, 2, block_in
    )
    block = turned.shape[3]
    halves = turned.reshape(turned.shape[0], turned.shape[1], 2, 2, block // 2)
    halves = lax.all_to_all(halves, "cores", split_axis=3, concat_axis=1, tiled=True)
    turned = halves.reshape(halves.shape[0], halves.shape[1], 2, block // 2)
    rows = turned.shape[1]
    matrix = jnp.transpose(turned, (3, 1, 2, 0)).reshape(turned.shape[3], rows, 2 * S)
    partial_value = cross_power(matrix)
    return (partial_value * norm_scale, phase_cal)


LANES = 128
VMEM_LIMIT = 56 * 1024 * 1024


def fast_tables():
    section_one, twist_cos, twist_sin, section_two = make_tables()
    first = section_one.reshape(2 * FA, FA)
    last = jnp.concatenate([section_two[0, :, 0], section_two[1, :, 0]], axis=0).T
    return first, twist_cos, twist_sin, last


def channelize_kernel(delay_ref, valid_ref, main_ref, next_ref, one_ref, cos_ref, sin_ref, two_ref,
                      out_ref, stream, twist_re, twist_im, turned):
    s = pl.program_id(0)
    stations = pl.num_programs(0)
    rows = 2 * FA
    stream[0:rows, :] = main_ref[0].astype(jnp.float32)
    stream[rows : rows + FA, :] = next_ref[0].astype(jnp.float32)
    delay = delay_ref[s]
    whole = delay // LANES
    part = delay % LANES
    lane = lax.broadcasted_iota(jnp.int32, (rows, LANES), 1)
    here = stream[pl.ds(whole, rows), :]
    after = stream[pl.ds(whole + 1, rows), :]
    mixed = jnp.where(lane < part, after, here)
    shifted = pltpu.roll(mixed, (LANES - part) % LANES, 1).astype(jnp.bfloat16)
    both = jnp.concatenate([shifted[:FA], shifted[FA:]], axis=1)
    section = jnp.dot(one_ref[...], both, preferred_element_type=jnp.float32)
    usable = valid_ref[s].astype(jnp.float32)
    cosine = cos_ref[...] * usable
    sine = sin_ref[...] * usable
    for t in range(2):
        re = section[:FA, t * LANES : (t + 1) * LANES]
        im = section[FA:, t * LANES : (t + 1) * LANES]
        twist_re[pl.ds(t * 32 + s, FA, stride=64), :] = re * cosine + im * sine
        twist_im[pl.ds(t * 32 + s, FA, stride=64), :] = im * cosine - re * sine

    @pl.when(s == stations - 1)
    def _():
        def second(k, carry):
            at = pl.multiple_of(k * 64, 64)
            re = twist_re[pl.ds(at, 64), :].astype(jnp.bfloat16)
            im = twist_im[pl.ds(at, 64), :].astype(jnp.bfloat16)
            right = jnp.concatenate(
                [jnp.concatenate([re, im], axis=1), jnp.concatenate([im, -re], axis=1)], axis=0
            )
            product = lax.dot_general(
                two_ref[...], right, (((1,), (1,)), ((), ())), preferred_element_type=jnp.float32
            )
            turned[pl.ds(k, FB // 2, stride=FA), :] = product
            return carry

        lax.fori_loop(0, FA, second, 0, unroll=8)

        def write(q, carry):
            at = pl.multiple_of(q * FA, FA)
            out_ref[q] = turned[pl.ds(at, FA), :].astype(jnp.bfloat16)
            return carry

        lax.fori_loop(0, FB // 2, write, 0, unroll=2)


def channelize_pair(pair, blocks, following, delays, valid, tables):
    first, twist_cos, twist_sin, last = tables
    source, next_at = following
    whole = lambda shape: pl.BlockSpec(shape, lambda s, *_: (0,) * len(shape))
    return pl.pallas_call(
        channelize_kernel,
        out_shape=jax.ShapeDtypeStruct((FB // 2, FA, LANES), jnp.bfloat16),
        grid_spec=pltpu.PrefetchScalarGridSpec(
            num_scalar_prefetch=2,
            grid=(blocks.shape[0],),
            in_specs=[
                pl.BlockSpec((1, 2 * FA, LANES), lambda s, *_: (s, pair, 0)),
                pl.BlockSpec((1, FA, LANES), lambda s, *_: (s, next_at, 0)),
                whole((2 * FA, FA)),
                whole((FA, FB)),
                whole((FA, FB)),
                whole((FB // 2, 2 * FB)),
            ],
            out_specs=whole((FB // 2, FA, LANES)),
            scratch_shapes=[
                pltpu.VMEM((3 * FA + 8, LANES), jnp.float32),
                pltpu.VMEM((FA * 64, LANES), jnp.float32),
                pltpu.VMEM((FA * 64, LANES), jnp.float32),
                pltpu.VMEM((FA * 64, LANES), jnp.float32),
            ],
        ),
        compiler_params=pltpu.CompilerParams(vmem_limit_bytes=VMEM_LIMIT),
        cost_estimate=pl.CostEstimate(
            flops=3 * 2 * 64 * 256 * 256 * 256, bytes_accessed=10 * 2**20, transcendentals=0
        ),
    )(delays, valid, blocks, source, first, twist_cos, twist_sin, last)


def exchange_kernel(sizes, zero_ref, one_ref, got_ref, local_sem, send_sem, recv_sem):
    n_stn, n_tm, n_cores = sizes
    n = n_stn * n_tm * n_cores
    me = (lax.axis_index("stn") * n_tm + lax.axis_index("tm")) * n_cores + lax.axis_index("cores")

    def place(device):
        return (device // (n_tm * n_cores), (device // n_cores) % n_tm, device % n_cores)

    barrier = pltpu.get_barrier_semaphore()

    def greet(k, carry):
        pl.semaphore_signal(
            barrier, inc=1, device_id=place((me + k) % n), device_id_type=pl.DeviceIdType.MESH
        )
        return carry

    lax.fori_loop(1, n, greet, 0)
    pl.semaphore_wait(barrier, n - 1)
    sources = (zero_ref, one_ref)

    def copy(pair, k):
        to = (me + k) % n
        return pltpu.make_async_remote_copy(
            src_ref=sources[pair].at[pl.ds(to * 2, 2)],
            dst_ref=got_ref.at[pair, me],
            send_sem=send_sem.at[pair, k],
            recv_sem=recv_sem.at[pair, k],
            device_id=place(to),
            device_id_type=pl.DeviceIdType.MESH,
        )

    for pair in range(2):
        lax.fori_loop(1, n, lambda k, carry, pair=pair: (copy(pair, k).start(), carry)[1], 0)
    own = [
        pltpu.make_async_copy(
            sources[pair].at[pl.ds(me * 2, 2)], got_ref.at[pair, me], local_sem.at[pair]
        )
        for pair in range(2)
    ]
    for one in own:
        one.start()
    for one in own:
        one.wait()
    for pair in range(2):
        lax.fori_loop(1, n, lambda k, carry, pair=pair: (copy(pair, k).wait(), carry)[1], 0)


def exchange(zero, one, sizes):
    n = math.prod(sizes)
    return pl.pallas_call(
        lambda *refs: exchange_kernel(sizes, *refs),
        out_shape=jax.ShapeDtypeStruct((2, n, 2, FA, LANES), jnp.bfloat16),
        in_specs=[pl.BlockSpec(memory_space=pl.ANY)] * 2,
        out_specs=pl.BlockSpec(memory_space=pl.ANY),
        scratch_shapes=[
            pltpu.SemaphoreType.DMA((2,)),
            pltpu.SemaphoreType.DMA((2, n)),
            pltpu.SemaphoreType.DMA((2, n)),
        ],
        compiler_params=pltpu.CompilerParams(collective_id=0, has_side_effects=True),
    )(zero, one)


CB = 64


def tones_kernel(first_ref, tone_ref, got_ref, out_ref, total):
    step = pl.program_id(0)

    @pl.when(step == 0)
    def _():
        out_ref[...] = jnp.zeros_like(out_ref)

    lane = lax.broadcasted_iota(jnp.int32, (CB, LANES), 1)
    sums = []
    for y in range(2):
        acc = jnp.zeros((CB, LANES), jnp.float32)
        for u in range(2):
            for j in range(got_ref.shape[2]):
                acc = acc + got_ref[u, y, j].astype(jnp.float32)
        sums.append(acc + pltpu.roll(acc, 96, 1))
    total[...] = jnp.where(lane % 64 < 32, sums[0], pltpu.roll(sums[1], 32, 1))
    start = first_ref[0] + step * CB
    picked = out_ref[...]
    for c in range(CB):
        picked = picked + jnp.where(tone_ref[...] == start + c, total[c : c + 1, :], 0.0)
    out_ref[...] = picked


def tones(got, tone_lanes, first_channel):
    _, n_stn, n_time, channels, _ = got.shape
    return pl.pallas_call(
        tones_kernel,
        out_shape=jax.ShapeDtypeStruct((NTONE, LANES), jnp.float32),
        grid_spec=pltpu.PrefetchScalarGridSpec(
            num_scalar_prefetch=1,
            grid=(channels // CB,),
            in_specs=[
                pl.BlockSpec((NTONE, LANES), lambda i, *_: (0, 0)),
                pl.BlockSpec((2, n_stn, n_time, CB, LANES), lambda i, *_: (0, 0, 0, i, 0)),
            ],
            out_specs=pl.BlockSpec((NTONE, LANES), lambda i, *_: (0, 0)),
            scratch_shapes=[pltpu.VMEM((CB, LANES), jnp.float32)],
        ),
        compiler_params=pltpu.CompilerParams(vmem_limit_bytes=VMEM_LIMIT),
    )(first_channel, tone_lanes, got)


def correlate_kernel(scale, got_ref, out_ref, matrix, power, turned):
    lane = lax.broadcasted_iota(jnp.int32, (CB, LANES), 1)
    low = lane % 64 < 32
    n_time = got_ref.shape[2]
    rows = 4 * n_time
    for u in range(2):
        for j in range(n_time):
            y0 = got_ref[u, 0, j].astype(jnp.float32)
            y1 = got_ref[u, 1, j].astype(jnp.float32)
            t = (u * n_time + j) * 2
            matrix[pl.ds(t, CB, stride=rows), :] = jnp.where(low, y0, pltpu.roll(y1, 32, 1))
            matrix[pl.ds(t + 1, CB, stride=rows), :] = jnp.where(low, pltpu.roll(y0, 96, 1), y1)
    left = lax.broadcasted_iota(jnp.int32, (S, LANES), 1) < 64
    left_half = lax.broadcasted_iota(jnp.int32, (S // 2, LANES), 1) < 64

    def channel(c, carry):
        at = pl.multiple_of(c * rows, rows)
        values = matrix[pl.ds(at, rows), :].astype(jnp.bfloat16)
        gram = lax.dot_general(
            values, values, (((0,), (0,)), ((), ())), preferred_element_type=jnp.float32
        )
        upper = gram[:S] * scale
        lower = pltpu.roll(gram[S:] * scale, 64, 1)
        slot = pl.multiple_of((c % 8) * S, S)
        power[pl.ds(slot, S), :] = jnp.where(left, upper + lower, lower - upper)
        even = power[pl.ds(slot, S // 2, stride=2), :]
        odd = power[pl.ds(slot + 1, S // 2, stride=2), :]
        turned[pl.ds(c, S // 2, stride=CB), :] = jnp.where(left_half, even, pltpu.roll(odd, 64, 1))
        turned[pl.ds(S // 2 * CB + c, S // 2, stride=CB), :] = jnp.where(
            left_half, pltpu.roll(even, 64, 1), odd
        )
        return carry

    lax.fori_loop(0, CB, channel, 0, unroll=8)
    for tile in range(S):
        out_ref[:, tile * LANES : (tile + 1) * LANES] = turned[tile * CB : (tile + 1) * CB, :]


def correlate(got, scale):
    _, n_stn, n_time, channels, _ = got.shape
    return pl.pallas_call(
        lambda *refs: correlate_kernel(scale, *refs),
        out_shape=jax.ShapeDtypeStruct((channels, 2 * S * S), jnp.float32),
        grid=(channels // CB,),
        in_specs=[pl.BlockSpec((2, n_stn, n_time, CB, LANES), lambda i: (0, 0, 0, i, 0))],
        out_specs=pl.BlockSpec((CB, 2 * S * S), lambda i: (i, 0)),
        scratch_shapes=[
            pltpu.VMEM((CB * 4 * n_time, LANES), jnp.float32),
            pltpu.VMEM((8 * S, LANES), jnp.float32),
            pltpu.VMEM((S * CB, LANES), jnp.float32),
        ],
        compiler_params=pltpu.CompilerParams(vmem_limit_bytes=VMEM_LIMIT),
        cost_estimate=pl.CostEstimate(
            flops=2 * channels * 64 * 128 * 128, bytes_accessed=26 * 2**20, transcendentals=0
        ),
    )(got)


def fast_shards(samples, delays, valid, tone_chan):
    tables = fast_tables()
    sizes = tuple(lax.axis_size(name) for name in ("stn", "tm", "cores"))
    n_stn, n_tm, n_cores = sizes
    stations, stretch = samples.shape
    trailing = passed_along(samples[:, :MAXD], ("tm", "cores"), -1)
    blocks = samples.reshape(stations, stretch // LANES, LANES)
    zero = channelize_pair(0, blocks, (blocks, 2), delays, valid, tables)
    halo = trailing.reshape(stations, MAXD // LANES, LANES)
    one = channelize_pair(1, blocks, (halo, 0), delays, valid, tables)
    channels = NCH // (n_stn * n_tm * n_cores)
    got = exchange(zero, one, sizes).reshape(2, n_stn, n_tm * n_cores, channels, LANES)
    scale = 1.0 / math.sqrt(stretch // (FA * FB) * n_tm * n_cores)
    me = (lax.axis_index("stn") * n_tm + lax.axis_index("tm")) * n_cores + lax.axis_index("cores")
    everyone = lax.all_gather(tone_chan, "stn", axis=0, tiled=True)
    tone_lanes = jnp.concatenate([everyone.T, everyone.T], axis=1)
    picks = tones(got, tone_lanes, (me * channels).astype(jnp.int32)[None])
    picks = lax.psum(picks, ("stn", "tm", "cores")) * scale
    visibility = correlate(got, scale)
    mine = lax.dynamic_slice_in_dim(
        picks.reshape(NTONE, 2, S), lax.axis_index("stn") * stations, stations, axis=2
    )
    phase_cal = jnp.transpose(mine, (2, 1, 0)).reshape(stations, 2 * NTONE)
    return (visibility, phase_cal)


def solution(mesh):
    sizes = mesh.shape
    body = fast_shards if sizes["stn"] == 2 and math.prod(sizes.values()) == 32 else shards
    return jax.shard_map(
        body,
        mesh=mesh,
        in_specs=(P("stn", ("tm", "cores")), P("stn"), P("stn"), P("stn", None)),
        out_specs=(P(("stn", "tm", "cores"), None), P("stn", None)),
        check_vma=False,
    )
```

```python
import math

import jax
import jax.numpy as jnp
from jax import lax
from jax.experimental import pallas as pl
from jax.experimental.pallas import tpu as pltpu
from jax.sharding import PartitionSpec as P

S = 64
NCH = 16384
FA = 256
FB = 128
NTONE = 64
MAXD = 32768


def passed_along(block, axis, distance):
    devices = range(lax.axis_size(axis))
    route = [(i - distance, i) for i in devices if i - distance in devices]
    return lax.ppermute(block, axis, route)


def make_tables():
    outer_idx = jnp.arange(FA, dtype=jnp.int32)
    phases = outer_idx[:, None] * outer_idx[None, :] % FA
    angles = 2.0 * math.pi / FA * phases.astype(jnp.float32)
    section_one = jnp.stack([jnp.cos(angles), -jnp.sin(angles)]).astype(jnp.bfloat16)
    inner_idx = jnp.arange(FB, dtype=jnp.int32)
    spectrum_len = FA * FB
    twist_idx = outer_idx[:, None] * inner_idx[None, :] % spectrum_len
    twists = 2.0 * math.pi / spectrum_len * twist_idx.astype(jnp.float32)
    norm_scale = 1.0 / math.sqrt(spectrum_len)
    twist_cos = jnp.cos(twists) * norm_scale
    twist_sin = jnp.sin(twists) * norm_scale
    half_idx = jnp.arange(FB // 2, dtype=jnp.int32)
    last_idx = inner_idx[:, None] * half_idx[None, :] % FB
    thetas = 2.0 * math.pi / FB * last_idx.astype(jnp.float32)
    cosine = jnp.cos(thetas)
    sine_val = jnp.sin(thetas)
    section_two = jnp.stack(
        [jnp.stack([cosine, -sine_val], axis=1), jnp.stack([sine_val, cosine], axis=1)]
    ).astype(jnp.bfloat16)
    return (section_one, twist_cos, twist_sin, section_two)


def channelize(window, usable, tables):
    section_one, twist_cos, twist_sin, section_two = tables
    spec_count = window.shape[0] // (FA * FB)
    blocks = window.reshape(spec_count, FA, FB)
    section_out = jnp.einsum(
        "xkn,bnm->bxkm", section_one, blocks, preferred_element_type=jnp.float32
    )
    real_part = section_out[:, 0] * twist_cos + section_out[:, 1] * twist_sin
    imag_part = section_out[:, 1] * twist_cos - section_out[:, 0] * twist_sin
    twisted = jnp.stack([real_part, imag_part], axis=1).astype(jnp.bfloat16)
    product = jnp.einsum(
        "xnrq,bxkn->brqk", section_two, twisted, preferred_element_type=jnp.float32
    )
    return (product.reshape(spec_count, 2, NCH) * usable).astype(jnp.bfloat16)


def cross_power(matrix):
    gram = jnp.einsum("cta,ctb->cab", matrix, matrix, preferred_element_type=jnp.float32)
    real_re = gram[:, :S, :S]
    imag_im = gram[:, S:, S:]
    imag_re = gram[:, S:, :S]
    real_im = gram[:, :S, S:]
    channels = gram.shape[0]
    first = (real_re + imag_im).reshape(channels, S * S)
    second = (imag_re - real_im).reshape(channels, S * S)
    return jnp.concatenate([first, second], axis=1)


def shards(samples, delays, valid, tone_chan):
    tables = make_tables()
    stretch = samples.shape[1]
    spectrum_len = FA * FB
    trailing = passed_along(samples[:, :MAXD], ("tm", "cores"), -1)
    extended = jnp.concatenate([samples, trailing], axis=1)
    chan_ids = jnp.arange(NCH, dtype=jnp.int32)

    def station(inputs):
        stream, shift_by, usable, tone_ids = inputs
        window = lax.dynamic_slice_in_dim(stream, shift_by, stretch)
        spectra = channelize(window, usable.astype(jnp.float32), tables)
        totals = jnp.sum(spectra, axis=0, dtype=jnp.float32)
        selector = (chan_ids[:, None] == tone_ids[None, :]).astype(jnp.float32)
        picked = jnp.dot(
            totals, selector, precision=lax.Precision.HIGHEST, preferred_element_type=jnp.float32
        )
        return (spectra, picked.reshape(2 * NTONE))

    spectra, tone_picks = lax.map(station, (extended, delays, valid, tone_chan))
    spectra_all = stretch // spectrum_len * lax.axis_size("tm") * lax.axis_size("cores")
    norm_scale = 1.0 / math.sqrt(spectra_all)
    phase_cal = lax.psum(tone_picks, ("tm", "cores")) * norm_scale
    local_stn = spectra.shape[0]
    spec_here = spectra.shape[1]
    n_stn = lax.axis_size("stn")
    n_tm = lax.axis_size("tm")
    received = lax.all_to_all(spectra[None], ("stn", "tm"), split_axis=4, concat_axis=0, tiled=True)
    block_in = received.shape[4]
    arranged = received.reshape(n_stn, n_tm, local_stn, spec_here, 2, block_in)
    turned = jnp.transpose(arranged, (0, 2, 1, 3, 4, 5)).reshape(
        n_stn * local_stn, n_tm * spec_here, 2, block_in
    )
    block = turned.shape[3]
    halves = turned.reshape(turned.shape[0], turned.shape[1], 2, 2, block // 2)
    halves = lax.all_to_all(halves, "cores", split_axis=3, concat_axis=1, tiled=True)
    turned = halves.reshape(halves.shape[0], halves.shape[1], 2, block // 2)
    rows = turned.shape[1]
    matrix = jnp.transpose(turned, (3, 1, 2, 0)).reshape(turned.shape[3], rows, 2 * S)
    partial_value = cross_power(matrix)
    return (partial_value * norm_scale, phase_cal)


LANES = 128
VMEM_LIMIT = 56 * 1024 * 1024


def fast_tables():
    section_one, twist_cos, twist_sin, section_two = make_tables()
    first = section_one.reshape(2 * FA, FA)
    last = jnp.concatenate([section_two[0, :, 0], section_two[1, :, 0]], axis=0).T
    return first, twist_cos, twist_sin, last


def first_stage(s, delay, usable, one_ref, cos_ref, sin_ref, stream, twist_re, twist_im):
    rows = 2 * FA
    whole = delay // LANES
    part = delay % LANES
    lane = lax.broadcasted_iota(jnp.int32, (rows, LANES), 1)
    here = stream[pl.ds(whole, rows), :]
    after = stream[pl.ds(whole + 1, rows), :]
    mixed = jnp.where(lane < part, after, here)
    shifted = pltpu.roll(mixed, (LANES - part) % LANES, 1).astype(jnp.bfloat16)
    both = jnp.concatenate([shifted[:FA], shifted[FA:]], axis=1)
    section = jnp.dot(one_ref[...], both, preferred_element_type=jnp.float32)
    cosine = cos_ref[...] * usable
    sine = sin_ref[...] * usable
    for t in range(2):
        re = section[:FA, t * LANES : (t + 1) * LANES]
        im = section[FA:, t * LANES : (t + 1) * LANES]
        twist_re[pl.ds(t * 32 + s, FA, stride=PITCH), :] = re * cosine + im * sine
        twist_im[pl.ds(t * 32 + s, FA, stride=PITCH), :] = im * cosine - re * sine


def second_stage(two_ref, out_ref, twist_re, twist_im, turned):
    def second(k, carry):
        re = twist_re[pl.ds(k * PITCH, 64), :].astype(jnp.bfloat16)
        im = twist_im[pl.ds(k * PITCH, 64), :].astype(jnp.bfloat16)
        right = jnp.concatenate(
            [jnp.concatenate([re, im], axis=1), jnp.concatenate([im, -re], axis=1)], axis=0
        )
        product = lax.dot_general(
            two_ref[...], right, (((1,), (1,)), ((), ())), preferred_element_type=jnp.float32
        )
        turned[pl.ds(k, FB // 2, stride=FA + 1), :] = product
        return carry

    lax.fori_loop(0, FA, second, 0, unroll=8)

    def write(q, carry):
        out_ref[q] = turned[pl.ds(q * (FA + 1), FA), :].astype(jnp.bfloat16)
        return carry

    lax.fori_loop(0, FB // 2, write, 0, unroll=2)


PITCH = 65
STAGE_SCRATCH = [
    pltpu.VMEM((3 * FA + 8, LANES), jnp.float32),
    pltpu.VMEM((FA * PITCH + 7, LANES), jnp.float32),
    pltpu.VMEM((FA * PITCH + 7, LANES), jnp.float32),
    pltpu.VMEM(((FA + 1) * FB // 2, LANES), jnp.float32),
]


def channelize_kernel(delay_ref, valid_ref, main_ref, next_ref, one_ref, cos_ref, sin_ref, two_ref,
                      out_ref, stream, twist_re, twist_im, turned):
    s = pl.program_id(0)
    rows = 2 * FA
    stream[0:rows, :] = main_ref[0].astype(jnp.float32)
    stream[rows : rows + FA, :] = next_ref[0].astype(jnp.float32)
    first_stage(s, delay_ref[s], valid_ref[s].astype(jnp.float32), one_ref, cos_ref, sin_ref,
                stream, twist_re, twist_im)

    @pl.when(s == pl.num_programs(0) - 1)
    def _():
        second_stage(two_ref, out_ref, twist_re, twist_im, turned)


def channelize_pair(pair, blocks, following, delays, valid, tables):
    first, twist_cos, twist_sin, last = tables
    source, next_at = following
    whole = lambda shape: pl.BlockSpec(shape, lambda s, *_: (0,) * len(shape))
    return pl.pallas_call(
        channelize_kernel,
        out_shape=jax.ShapeDtypeStruct((FB // 2, FA, LANES), jnp.bfloat16),
        grid_spec=pltpu.PrefetchScalarGridSpec(
            num_scalar_prefetch=2,
            grid=(blocks.shape[0],),
            in_specs=[
                pl.BlockSpec((1, 2 * FA, LANES), lambda s, *_: (s, pair, 0)),
                pl.BlockSpec((1, FA, LANES), lambda s, *_: (s, next_at, 0)),
                whole((2 * FA, FA)),
                whole((FA, FB)),
                whole((FA, FB)),
                whole((FB // 2, 2 * FB)),
            ],
            out_specs=whole((FB // 2, FA, LANES)),
            scratch_shapes=STAGE_SCRATCH,
        ),
        compiler_params=pltpu.CompilerParams(vmem_limit_bytes=VMEM_LIMIT),
        cost_estimate=pl.CostEstimate(
            flops=3 * 2 * 64 * 256 * 256 * 256, bytes_accessed=10 * 2**20, transcendentals=0
        ),
    )(delays, valid, blocks, source, first, twist_cos, twist_sin, last)


def linear_index(sizes):
    n_stn, n_tm, n_cores = sizes
    return (lax.axis_index("stn") * n_tm + lax.axis_index("tm")) * n_cores + lax.axis_index("cores")


def exchange_kernel(sizes, zero_ref, delay_ref, valid_ref, main_ref, next_ref, one_ref, cos_ref,
                    sin_ref, two_ref, got_ref, stream, twist_re, twist_im, turned, later,
                    local_sem, send_sem, recv_sem):
    _, n_tm, n_cores = sizes
    n = math.prod(sizes)
    me = linear_index(sizes)

    def place(device):
        return (device // (n_tm * n_cores), (device // n_cores) % n_tm, device % n_cores)

    barrier = pltpu.get_barrier_semaphore()

    def greet(k, carry):
        pl.semaphore_signal(
            barrier, inc=1, device_id=place((me + k) % n), device_id_type=pl.DeviceIdType.MESH
        )
        return carry

    lax.fori_loop(1, n, greet, 0)
    pl.semaphore_wait(barrier, n - 1)
    sources = (zero_ref, later)

    def copy(pair, k):
        to = (me + k) % n
        return pltpu.make_async_remote_copy(
            src_ref=sources[pair].at[pl.ds(to * 2, 2)],
            dst_ref=got_ref.at[pair, me],
            send_sem=send_sem.at[pair, k],
            recv_sem=recv_sem.at[pair, k],
            device_id=place(to),
            device_id_type=pl.DeviceIdType.MESH,
        )

    def own(pair):
        return pltpu.make_async_copy(
            sources[pair].at[pl.ds(me * 2, 2)], got_ref.at[pair, me], local_sem.at[pair]
        )

    def send(pair):
        lax.fori_loop(1, n, lambda k, carry: (copy(pair, k).start(), carry)[1], 0)
        own(pair).start()

    def finish(pair):
        own(pair).wait()
        lax.fori_loop(1, n, lambda k, carry: (copy(pair, k).wait(), carry)[1], 0)

    send(0)

    def station(s, carry):
        rows = 2 * FA
        stream[0:rows, :] = main_ref[s].astype(jnp.float32)
        stream[rows : rows + FA, :] = next_ref[s].astype(jnp.float32)
        first_stage(s, delay_ref[s], valid_ref[s].astype(jnp.float32), one_ref, cos_ref, sin_ref,
                    stream, twist_re, twist_im)
        return carry

    lax.fori_loop(0, main_ref.shape[0], station, 0)
    second_stage(two_ref, later, twist_re, twist_im, turned)
    send(1)
    finish(0)
    finish(1)


def exchange(zero, blocks, halo, delays, valid, tables, sizes):
    n = math.prod(sizes)
    stations = blocks.shape[0]
    whole = lambda shape: pl.BlockSpec(shape, lambda i: (0,) * len(shape))
    smem = pl.BlockSpec(memory_space=pltpu.SMEM)
    return pl.pallas_call(
        lambda *refs: exchange_kernel(sizes, *refs),
        out_shape=jax.ShapeDtypeStruct((2, n, 2, FA, LANES), jnp.bfloat16),
        grid=(1,),
        in_specs=[
            pl.BlockSpec(memory_space=pl.ANY),
            smem,
            smem,
            pl.BlockSpec((stations, 2 * FA, LANES), lambda i: (0, 1, 0)),
            whole((stations, FA, LANES)),
            whole((2 * FA, FA)),
            whole((FA, FB)),
            whole((FA, FB)),
            whole((FB // 2, 2 * FB)),
        ],
        out_specs=pl.BlockSpec(memory_space=pl.ANY),
        scratch_shapes=STAGE_SCRATCH
        + [
            pltpu.VMEM((FB // 2, FA, LANES), jnp.bfloat16),
            pltpu.SemaphoreType.DMA((2,)),
            pltpu.SemaphoreType.DMA((2, n)),
            pltpu.SemaphoreType.DMA((2, n)),
        ],
        compiler_params=pltpu.CompilerParams(
            collective_id=0, has_side_effects=True, vmem_limit_bytes=VMEM_LIMIT
        ),
    )(zero, delays, valid, blocks, halo, *tables)


CB = 64


def tones_kernel(sizes, scale, tone_ref, got_ref, out_ref, total, picks, sent, arrived, send_sem, recv_sem):
    step = pl.program_id(0)
    steps = pl.num_programs(0)
    me = linear_index(sizes)

    @pl.when(step == 0)
    def _():
        picks[...] = jnp.zeros_like(picks)

    lane = lax.broadcasted_iota(jnp.int32, (CB, LANES), 1)
    sums = []
    for y in range(2):
        acc = jnp.zeros((CB, LANES), jnp.float32)
        for u in range(2):
            for j in range(got_ref.shape[2]):
                acc = acc + got_ref[u, y, j].astype(jnp.float32)
        sums.append(acc + pltpu.roll(acc, 96, 1))
    total[...] = jnp.where(lane % 64 < 32, sums[0], pltpu.roll(sums[1], 32, 1))
    start = (me * steps + step) * CB
    picked = picks[...]
    for c in range(CB):
        picked = picked + jnp.where(tone_ref[...] == start + c, total[c : c + 1, :], 0.0)
    picks[...] = picked

    @pl.when(step == steps - 1)
    def _():
        flips = []
        for name, size in zip(("cores", "stn", "tm"), (sizes[2], sizes[0], sizes[1])):
            bit = 1
            while bit < size:
                at = lax.axis_index(name)
                flips.append({name: at + bit * (1 - 2 * ((at // bit) % 2))})
                bit *= 2
        barrier = pltpu.get_barrier_semaphore()
        for partner in flips:
            pl.semaphore_signal(
                barrier, inc=1, device_id=partner, device_id_type=pl.DeviceIdType.MESH
            )
        pl.semaphore_wait(barrier, len(flips))
        running = picks[...]
        for r, partner in enumerate(flips):
            sent[r] = running
            copy = pltpu.make_async_remote_copy(
                src_ref=sent.at[r],
                dst_ref=arrived.at[r],
                send_sem=send_sem.at[r],
                recv_sem=recv_sem.at[r],
                device_id=partner,
                device_id_type=pl.DeviceIdType.MESH,
            )
            copy.start()
            copy.wait()
            running = running + arrived[r]
        out_ref[...] = running * scale


def tones(got, tone_lanes, sizes, scale):
    _, n_stn, n_time, channels, _ = got.shape
    rounds = math.prod(sizes).bit_length() - 1
    return pl.pallas_call(
        lambda *refs: tones_kernel(sizes, scale, *refs),
        out_shape=jax.ShapeDtypeStruct((NTONE, LANES), jnp.float32),
        grid=(channels // CB,),
        in_specs=[
            pl.BlockSpec((NTONE, LANES), lambda i: (0, 0)),
            pl.BlockSpec((2, n_stn, n_time, CB, LANES), lambda i: (0, 0, 0, i, 0)),
        ],
        out_specs=pl.BlockSpec((NTONE, LANES), lambda i: (0, 0)),
        scratch_shapes=[
            pltpu.VMEM((CB, LANES), jnp.float32),
            pltpu.VMEM((NTONE, LANES), jnp.float32),
            pltpu.VMEM((rounds, NTONE, LANES), jnp.float32),
            pltpu.VMEM((rounds, NTONE, LANES), jnp.float32),
            pltpu.SemaphoreType.DMA((rounds,)),
            pltpu.SemaphoreType.DMA((rounds,)),
        ],
        compiler_params=pltpu.CompilerParams(
            collective_id=1, has_side_effects=True, vmem_limit_bytes=VMEM_LIMIT
        ),
    )(tone_lanes, got)


def correlate_kernel(scale, got_ref, out_ref, matrix, power, turned):
    lane = lax.broadcasted_iota(jnp.int32, (CB, LANES), 1)
    low = lane % 64 < 32
    n_time = got_ref.shape[2]
    rows = 4 * n_time
    pitch = rows + 1
    for u in range(2):
        for j in range(n_time):
            y0 = got_ref[u, 0, j].astype(jnp.float32)
            y1 = got_ref[u, 1, j].astype(jnp.float32)
            t = (u * n_time + j) * 2
            matrix[pl.ds(t, CB, stride=pitch), :] = jnp.where(low, y0, pltpu.roll(y1, 32, 1))
            matrix[pl.ds(t + 1, CB, stride=pitch), :] = jnp.where(low, pltpu.roll(y0, 96, 1), y1)
    left = lax.broadcasted_iota(jnp.int32, (S, LANES), 1) < 64
    left_half = lax.broadcasted_iota(jnp.int32, (S // 2, LANES), 1) < 64

    def channel(c, carry):
        values = matrix[pl.ds(c * pitch, rows), :].astype(jnp.bfloat16)
        gram = lax.dot_general(
            values, values, (((0,), (0,)), ((), ())), preferred_element_type=jnp.float32
        )
        upper = gram[:S] * scale
        lower = pltpu.roll(gram[S:] * scale, 64, 1)
        slot = pl.multiple_of((c % 8) * S, S)
        power[pl.ds(slot, S), :] = jnp.where(left, upper + lower, lower - upper)
        even = power[pl.ds(slot, S // 2, stride=2), :]
        odd = power[pl.ds(slot + 1, S // 2, stride=2), :]
        turned[pl.ds(c, S // 2, stride=CB + 1), :] = jnp.where(left_half, even, pltpu.roll(odd, 64, 1))
        turned[pl.ds(S // 2 * (CB + 1) + c, S // 2, stride=CB + 1), :] = jnp.where(
            left_half, pltpu.roll(even, 64, 1), odd
        )
        return carry

    lax.fori_loop(0, CB, channel, 0, unroll=8)
    for tile in range(S):
        at = tile * (CB + 1)
        out_ref[:, tile * LANES : (tile + 1) * LANES] = turned[at : at + CB, :]


def correlate(got, scale):
    _, n_stn, n_time, channels, _ = got.shape
    return pl.pallas_call(
        lambda *refs: correlate_kernel(scale, *refs),
        out_shape=jax.ShapeDtypeStruct((channels, 2 * S * S), jnp.float32),
        grid=(channels // CB,),
        in_specs=[pl.BlockSpec((2, n_stn, n_time, CB, LANES), lambda i: (0, 0, 0, i, 0))],
        out_specs=pl.BlockSpec((CB, 2 * S * S), lambda i: (i, 0)),
        scratch_shapes=[
            pltpu.VMEM((CB * (4 * n_time + 1), LANES), jnp.float32),
            pltpu.VMEM((8 * S, LANES), jnp.float32),
            pltpu.VMEM((S * (CB + 1), LANES), jnp.float32),
        ],
        compiler_params=pltpu.CompilerParams(vmem_limit_bytes=VMEM_LIMIT),
        cost_estimate=pl.CostEstimate(
            flops=2 * channels * 64 * 128 * 128, bytes_accessed=26 * 2**20, transcendentals=0
        ),
    )(got)


def fast_shards(samples, delays, valid, tone_chan):
    tables = fast_tables()
    sizes = tuple(lax.axis_size(name) for name in ("stn", "tm", "cores"))
    n_stn, n_tm, n_cores = sizes
    stations, stretch = samples.shape
    trailing = passed_along(samples[:, :MAXD], ("tm", "cores"), -1)
    blocks = samples.reshape(stations, stretch // LANES, LANES)
    zero = channelize_pair(0, blocks, (blocks, 2), delays, valid, tables)
    halo = trailing.reshape(stations, MAXD // LANES, LANES)
    channels = NCH // math.prod(sizes)
    got = exchange(zero, blocks, halo, delays, valid, tables, sizes)
    got = got.reshape(2, n_stn, n_tm * n_cores, channels, LANES)
    scale = 1.0 / math.sqrt(stretch // (FA * FB) * n_tm * n_cores)
    everyone = lax.all_gather(tone_chan, "stn", axis=0, tiled=True)
    tone_lanes = jnp.concatenate([everyone.T, everyone.T], axis=1)
    picks = tones(got, tone_lanes, sizes, scale)
    visibility = correlate(got, scale)
    mine = lax.dynamic_slice_in_dim(
        picks.reshape(NTONE, 2, S), lax.axis_index("stn") * stations, stations, axis=2
    )
    phase_cal = jnp.transpose(mine, (2, 1, 0)).reshape(stations, 2 * NTONE)
    return (visibility, phase_cal)


def solution(mesh):
    sizes = mesh.shape
    body = fast_shards if sizes["stn"] == 2 and math.prod(sizes.values()) == 32 else shards
    return jax.shard_map(
        body,
        mesh=mesh,
        in_specs=(P("stn", ("tm", "cores")), P("stn"), P("stn"), P("stn", None)),
        out_specs=(P(("stn", "tm", "cores"), None), P("stn", None)),
        check_vma=False,
    )
```

```python
import math

import jax
import jax.numpy as jnp
import ml_dtypes
import numpy as np
from jax import lax
from jax.experimental import pallas as pl
from jax.experimental.pallas import tpu as pltpu
from jax.sharding import PartitionSpec as P

S = 64
NCH = 16384
FA = 256
FB = 128
NTONE = 64
MAXD = 32768


def passed_along(block, axis, distance):
    devices = range(lax.axis_size(axis))
    route = [(i - distance, i) for i in devices if i - distance in devices]
    return lax.ppermute(block, axis, route)


def make_tables():
    outer_idx = jnp.arange(FA, dtype=jnp.int32)
    phases = outer_idx[:, None] * outer_idx[None, :] % FA
    angles = 2.0 * math.pi / FA * phases.astype(jnp.float32)
    section_one = jnp.stack([jnp.cos(angles), -jnp.sin(angles)]).astype(jnp.bfloat16)
    inner_idx = jnp.arange(FB, dtype=jnp.int32)
    spectrum_len = FA * FB
    twist_idx = outer_idx[:, None] * inner_idx[None, :] % spectrum_len
    twists = 2.0 * math.pi / spectrum_len * twist_idx.astype(jnp.float32)
    norm_scale = 1.0 / math.sqrt(spectrum_len)
    twist_cos = jnp.cos(twists) * norm_scale
    twist_sin = jnp.sin(twists) * norm_scale
    half_idx = jnp.arange(FB // 2, dtype=jnp.int32)
    last_idx = inner_idx[:, None] * half_idx[None, :] % FB
    thetas = 2.0 * math.pi / FB * last_idx.astype(jnp.float32)
    cosine = jnp.cos(thetas)
    sine_val = jnp.sin(thetas)
    section_two = jnp.stack(
        [jnp.stack([cosine, -sine_val], axis=1), jnp.stack([sine_val, cosine], axis=1)]
    ).astype(jnp.bfloat16)
    return (section_one, twist_cos, twist_sin, section_two)


def channelize(window, usable, tables):
    section_one, twist_cos, twist_sin, section_two = tables
    spec_count = window.shape[0] // (FA * FB)
    blocks = window.reshape(spec_count, FA, FB)
    section_out = jnp.einsum(
        "xkn,bnm->bxkm", section_one, blocks, preferred_element_type=jnp.float32
    )
    real_part = section_out[:, 0] * twist_cos + section_out[:, 1] * twist_sin
    imag_part = section_out[:, 1] * twist_cos - section_out[:, 0] * twist_sin
    twisted = jnp.stack([real_part, imag_part], axis=1).astype(jnp.bfloat16)
    product = jnp.einsum(
        "xnrq,bxkn->brqk", section_two, twisted, preferred_element_type=jnp.float32
    )
    return (product.reshape(spec_count, 2, NCH) * usable).astype(jnp.bfloat16)


def cross_power(matrix):
    gram = jnp.einsum("cta,ctb->cab", matrix, matrix, preferred_element_type=jnp.float32)
    real_re = gram[:, :S, :S]
    imag_im = gram[:, S:, S:]
    imag_re = gram[:, S:, :S]
    real_im = gram[:, :S, S:]
    channels = gram.shape[0]
    first = (real_re + imag_im).reshape(channels, S * S)
    second = (imag_re - real_im).reshape(channels, S * S)
    return jnp.concatenate([first, second], axis=1)


def shards(samples, delays, valid, tone_chan):
    tables = make_tables()
    stretch = samples.shape[1]
    spectrum_len = FA * FB
    trailing = passed_along(samples[:, :MAXD], ("tm", "cores"), -1)
    extended = jnp.concatenate([samples, trailing], axis=1)
    chan_ids = jnp.arange(NCH, dtype=jnp.int32)

    def station(inputs):
        stream, shift_by, usable, tone_ids = inputs
        window = lax.dynamic_slice_in_dim(stream, shift_by, stretch)
        spectra = channelize(window, usable.astype(jnp.float32), tables)
        totals = jnp.sum(spectra, axis=0, dtype=jnp.float32)
        selector = (chan_ids[:, None] == tone_ids[None, :]).astype(jnp.float32)
        picked = jnp.dot(
            totals, selector, precision=lax.Precision.HIGHEST, preferred_element_type=jnp.float32
        )
        return (spectra, picked.reshape(2 * NTONE))

    spectra, tone_picks = lax.map(station, (extended, delays, valid, tone_chan))
    spectra_all = stretch // spectrum_len * lax.axis_size("tm") * lax.axis_size("cores")
    norm_scale = 1.0 / math.sqrt(spectra_all)
    phase_cal = lax.psum(tone_picks, ("tm", "cores")) * norm_scale
    local_stn = spectra.shape[0]
    spec_here = spectra.shape[1]
    n_stn = lax.axis_size("stn")
    n_tm = lax.axis_size("tm")
    received = lax.all_to_all(spectra[None], ("stn", "tm"), split_axis=4, concat_axis=0, tiled=True)
    block_in = received.shape[4]
    arranged = received.reshape(n_stn, n_tm, local_stn, spec_here, 2, block_in)
    turned = jnp.transpose(arranged, (0, 2, 1, 3, 4, 5)).reshape(
        n_stn * local_stn, n_tm * spec_here, 2, block_in
    )
    block = turned.shape[3]
    halves = turned.reshape(turned.shape[0], turned.shape[1], 2, 2, block // 2)
    halves = lax.all_to_all(halves, "cores", split_axis=3, concat_axis=1, tiled=True)
    turned = halves.reshape(halves.shape[0], halves.shape[1], 2, block // 2)
    rows = turned.shape[1]
    matrix = jnp.transpose(turned, (3, 1, 2, 0)).reshape(turned.shape[3], rows, 2 * S)
    partial_value = cross_power(matrix)
    return (partial_value * norm_scale, phase_cal)


LANES = 128
VMEM_LIMIT = 56 * 1024 * 1024


def fast_tables():
    def turn(left, right, period):
        angle = np.float32(2.0 * math.pi / period)
        phases = (np.arange(left)[:, None] * np.arange(right)[None, :] % period).astype(np.float32)
        return np.cos(angle * phases), np.sin(angle * phases)

    cosine, sine = turn(FA, FA, FA)
    first = np.concatenate([cosine, -sine], axis=0).astype(ml_dtypes.bfloat16)
    cosine, sine = turn(FA, FB, FA * FB)
    norm_scale = np.float32(1.0 / math.sqrt(FA * FB))
    twist_cos, twist_sin = cosine * norm_scale, sine * norm_scale
    cosine, sine = turn(FB // 2, FB, FB)
    last = np.concatenate([cosine, sine], axis=1).astype(ml_dtypes.bfloat16)
    return tuple(jnp.asarray(table) for table in (first, twist_cos, twist_sin, last))


def first_stage(s, delay, usable, one_ref, cos_ref, sin_ref, stream, twist_re, twist_im):
    rows = 2 * FA
    whole = delay // LANES
    part = delay % LANES
    lane = lax.broadcasted_iota(jnp.int32, (rows, LANES), 1)
    here = stream[pl.ds(whole, rows), :]
    after = stream[pl.ds(whole + 1, rows), :]
    mixed = jnp.where(lane < part, after, here)
    shifted = pltpu.roll(mixed, (LANES - part) % LANES, 1).astype(jnp.bfloat16)
    both = jnp.concatenate([shifted[:FA], shifted[FA:]], axis=1)
    section = jnp.dot(one_ref[...], both, preferred_element_type=jnp.float32)
    cosine = cos_ref[...] * usable
    sine = sin_ref[...] * usable
    for t in range(2):
        re = section[:FA, t * LANES : (t + 1) * LANES]
        im = section[FA:, t * LANES : (t + 1) * LANES]
        twist_re[pl.ds(t * 32 + s, FA, stride=PITCH), :] = re * cosine + im * sine
        twist_im[pl.ds(t * 32 + s, FA, stride=PITCH), :] = im * cosine - re * sine


def second_stage(two_ref, out_ref, twist_re, twist_im, turned):
    def second(k, carry):
        re = twist_re[pl.ds(k * PITCH, 64), :].astype(jnp.bfloat16)
        im = twist_im[pl.ds(k * PITCH, 64), :].astype(jnp.bfloat16)
        right = jnp.concatenate(
            [jnp.concatenate([re, im], axis=1), jnp.concatenate([im, -re], axis=1)], axis=0
        )
        product = lax.dot_general(
            two_ref[...], right, (((1,), (1,)), ((), ())), preferred_element_type=jnp.float32
        )
        turned[pl.ds(k, FB // 2, stride=FA + 1), :] = product
        return carry

    lax.fori_loop(0, FA, second, 0, unroll=8)

    def write(q, carry):
        out_ref[q] = turned[pl.ds(q * (FA + 1), FA), :].astype(jnp.bfloat16)
        return carry

    lax.fori_loop(0, FB // 2, write, 0, unroll=2)


PITCH = 65
STAGE_SCRATCH = [
    pltpu.VMEM((3 * FA + 8, LANES), jnp.float32),
    pltpu.VMEM((FA * PITCH + 7, LANES), jnp.float32),
    pltpu.VMEM((FA * PITCH + 7, LANES), jnp.float32),
    pltpu.VMEM(((FA + 1) * FB // 2, LANES), jnp.float32),
]


def channelize_kernel(delay_ref, valid_ref, main_ref, next_ref, one_ref, cos_ref, sin_ref, two_ref,
                      out_ref, stream, twist_re, twist_im, turned):
    s = pl.program_id(0)
    rows = 2 * FA
    stream[0:rows, :] = main_ref[0].astype(jnp.float32)
    stream[rows : rows + FA, :] = next_ref[0].astype(jnp.float32)
    first_stage(s, delay_ref[s], valid_ref[s].astype(jnp.float32), one_ref, cos_ref, sin_ref,
                stream, twist_re, twist_im)

    @pl.when(s == pl.num_programs(0) - 1)
    def _():
        second_stage(two_ref, out_ref, twist_re, twist_im, turned)


def channelize_pair(pair, blocks, following, delays, valid, tables):
    first, twist_cos, twist_sin, last = tables
    source, next_at = following
    whole = lambda shape: pl.BlockSpec(shape, lambda s, *_: (0,) * len(shape))
    return pl.pallas_call(
        channelize_kernel,
        out_shape=jax.ShapeDtypeStruct((FB // 2, FA, LANES), jnp.bfloat16),
        grid_spec=pltpu.PrefetchScalarGridSpec(
            num_scalar_prefetch=2,
            grid=(blocks.shape[0],),
            in_specs=[
                pl.BlockSpec((1, 2 * FA, LANES), lambda s, *_: (s, pair, 0)),
                pl.BlockSpec((1, FA, LANES), lambda s, *_: (s, next_at, 0)),
                whole((2 * FA, FA)),
                whole((FA, FB)),
                whole((FA, FB)),
                whole((FB // 2, 2 * FB)),
            ],
            out_specs=whole((FB // 2, FA, LANES)),
            scratch_shapes=STAGE_SCRATCH,
        ),
        compiler_params=pltpu.CompilerParams(vmem_limit_bytes=VMEM_LIMIT),
        cost_estimate=pl.CostEstimate(
            flops=3 * 2 * 64 * 256 * 256 * 256, bytes_accessed=10 * 2**20, transcendentals=0
        ),
    )(delays, valid, blocks, source, first, twist_cos, twist_sin, last)


def linear_index(sizes):
    n_stn, n_tm, n_cores = sizes
    return (lax.axis_index("stn") * n_tm + lax.axis_index("tm")) * n_cores + lax.axis_index("cores")


def pick_tones(tone_ref, turned, picks, stations, first):
    lane = lax.broadcasted_iota(jnp.int32, (1, LANES), 1) % 32

    def tone(k, carry):
        row = jnp.zeros((1, LANES), jnp.float32)
        for s in range(stations):
            channel = tone_ref[s, k]
            row = jnp.where(lane == s, turned[pl.ds(channel + channel // FA, 1), :], row)
        row = row.astype(jnp.bfloat16).astype(jnp.float32)
        picks[pl.ds(k, 1), :] = row if first else picks[pl.ds(k, 1), :] + row
        return carry

    lax.fori_loop(0, NTONE, tone, 0)


def exchange_kernel(sizes, scale, zero_ref, delay_ref, valid_ref, tone_ref, main_ref, next_ref, one_ref,
                    cos_ref, sin_ref, two_ref, got_ref, tones_ref, stream, twist_re, twist_im,
                    turned, later, picks, sent, arrived, local_sem, send_sem, recv_sem, load_sem,
                    tone_send, tone_recv):
    _, n_tm, n_cores = sizes
    n = math.prod(sizes)
    me = linear_index(sizes)

    def place(device):
        return (device // (n_tm * n_cores), (device // n_cores) % n_tm, device % n_cores)

    barrier = pltpu.get_barrier_semaphore()

    def greet(k, carry):
        pl.semaphore_signal(
            barrier, inc=1, device_id=place((me + k) % n), device_id_type=pl.DeviceIdType.MESH
        )
        return carry

    lax.fori_loop(1, n, greet, 0)
    pl.semaphore_wait(barrier, n - 1)
    sources = (zero_ref, later)

    def copy(pair, k):
        to = (me + k) % n
        return pltpu.make_async_remote_copy(
            src_ref=sources[pair].at[pl.ds(to * 2, 2)],
            dst_ref=got_ref.at[pair, me],
            send_sem=send_sem.at[pair, k],
            recv_sem=recv_sem.at[pair, k],
            device_id=place(to),
            device_id_type=pl.DeviceIdType.MESH,
        )

    def own(pair):
        return pltpu.make_async_copy(
            sources[pair].at[pl.ds(me * 2, 2)], got_ref.at[pair, me], local_sem.at[pair]
        )

    def send(pair):
        lax.fori_loop(1, n, lambda k, carry: (copy(pair, k).start(), carry)[1], 0)
        own(pair).start()

    def finish(pair):
        own(pair).wait()
        lax.fori_loop(1, n, lambda k, carry: (copy(pair, k).wait(), carry)[1], 0)

    send(0)
    load = pltpu.make_async_copy(zero_ref, later, load_sem)
    load.start()
    load.wait()

    def widen(q, carry):
        turned[pl.ds(q * (FA + 1), FA), :] = later[q].astype(jnp.float32)
        return carry

    lax.fori_loop(0, FB // 2, widen, 0, unroll=2)
    stations = main_ref.shape[0]
    pick_tones(tone_ref, turned, picks, stations, True)

    def station(s, carry):
        rows = 2 * FA
        stream[0:rows, :] = main_ref[s].astype(jnp.float32)
        stream[rows : rows + FA, :] = next_ref[s].astype(jnp.float32)
        first_stage(s, delay_ref[s], valid_ref[s].astype(jnp.float32), one_ref, cos_ref, sin_ref,
                    stream, twist_re, twist_im)
        return carry

    lax.fori_loop(0, stations, station, 0)
    second_stage(two_ref, later, twist_re, twist_im, turned)
    send(1)
    pick_tones(tone_ref, turned, picks, stations, False)
    running = picks[...] + pltpu.roll(picks[...], 96, 1)
    flips = []
    for name, size in (("cores", n_cores), ("tm", n_tm)):
        bit = 1
        while bit < size:
            at = lax.axis_index(name)
            flips.append({name: at + bit * (1 - 2 * ((at // bit) % 2))})
            bit *= 2
    for r, partner in enumerate(flips):
        sent[r] = running
        passing = pltpu.make_async_remote_copy(
            src_ref=sent.at[r],
            dst_ref=arrived.at[r],
            send_sem=tone_send.at[r],
            recv_sem=tone_recv.at[r],
            device_id=partner,
            device_id_type=pl.DeviceIdType.MESH,
        )
        passing.start()
        passing.wait()
        running = running + arrived[r]
    tones_ref[...] = running * scale
    finish(0)
    finish(1)


def exchange(zero, blocks, halo, delays, valid, tone_chan, tables, sizes, scale):
    n = math.prod(sizes)
    rounds = (sizes[1] * sizes[2]).bit_length() - 1
    stations = blocks.shape[0]
    whole = lambda shape: pl.BlockSpec(shape, lambda i: (0,) * len(shape))
    smem = pl.BlockSpec(memory_space=pltpu.SMEM)
    return pl.pallas_call(
        lambda *refs: exchange_kernel(sizes, scale, *refs),
        out_shape=(
            jax.ShapeDtypeStruct((2, n, 2, FA, LANES), jnp.bfloat16),
            jax.ShapeDtypeStruct((NTONE, LANES), jnp.float32),
        ),
        grid=(1,),
        in_specs=[
            pl.BlockSpec(memory_space=pl.ANY),
            smem,
            smem,
            smem,
            pl.BlockSpec((stations, 2 * FA, LANES), lambda i: (0, 1, 0)),
            whole((stations, FA, LANES)),
            whole((2 * FA, FA)),
            whole((FA, FB)),
            whole((FA, FB)),
            whole((FB // 2, 2 * FB)),
        ],
        out_specs=(pl.BlockSpec(memory_space=pl.ANY), whole((NTONE, LANES))),
        scratch_shapes=STAGE_SCRATCH
        + [
            pltpu.VMEM((FB // 2, FA, LANES), jnp.bfloat16),
            pltpu.VMEM((NTONE, LANES), jnp.float32),
            pltpu.VMEM((rounds, NTONE, LANES), jnp.float32),
            pltpu.VMEM((rounds, NTONE, LANES), jnp.float32),
            pltpu.SemaphoreType.DMA((2,)),
            pltpu.SemaphoreType.DMA((2, n)),
            pltpu.SemaphoreType.DMA((2, n)),
            pltpu.SemaphoreType.DMA,
            pltpu.SemaphoreType.DMA((rounds,)),
            pltpu.SemaphoreType.DMA((rounds,)),
        ],
        compiler_params=pltpu.CompilerParams(
            collective_id=0, has_side_effects=True, vmem_limit_bytes=VMEM_LIMIT
        ),
    )(zero, delays, valid, tone_chan, blocks, halo, *tables)


CB = 64


def correlate_kernel(scale, got_ref, out_ref, matrix, power, turned):
    lane = lax.broadcasted_iota(jnp.int32, (CB, LANES), 1)
    low = lane % 64 < 32
    n_time = got_ref.shape[2]
    rows = 4 * n_time
    pitch = rows + 1
    for u in range(2):
        for j in range(n_time):
            y0 = got_ref[u, 0, j].astype(jnp.float32)
            y1 = got_ref[u, 1, j].astype(jnp.float32)
            t = (u * n_time + j) * 2
            matrix[pl.ds(t, CB, stride=pitch), :] = jnp.where(low, y0, pltpu.roll(y1, 32, 1))
            matrix[pl.ds(t + 1, CB, stride=pitch), :] = jnp.where(low, pltpu.roll(y0, 96, 1), y1)
    left = lax.broadcasted_iota(jnp.int32, (S, LANES), 1) < 64
    left_half = lax.broadcasted_iota(jnp.int32, (S // 2, LANES), 1) < 64

    def channel(c, carry):
        values = matrix[pl.ds(c * pitch, rows), :].astype(jnp.bfloat16)
        gram = lax.dot_general(
            values, values, (((0,), (0,)), ((), ())), preferred_element_type=jnp.float32
        )
        upper = gram[:S] * scale
        lower = pltpu.roll(gram[S:] * scale, 64, 1)
        slot = pl.multiple_of((c % 8) * S, S)
        power[pl.ds(slot, S), :] = jnp.where(left, upper + lower, lower - upper)
        even = power[pl.ds(slot, S // 2, stride=2), :]
        odd = power[pl.ds(slot + 1, S // 2, stride=2), :]
        turned[pl.ds(c, S // 2, stride=CB + 1), :] = jnp.where(left_half, even, pltpu.roll(odd, 64, 1))
        turned[pl.ds(S // 2 * (CB + 1) + c, S // 2, stride=CB + 1), :] = jnp.where(
            left_half, pltpu.roll(even, 64, 1), odd
        )
        return carry

    lax.fori_loop(0, CB, channel, 0, unroll=8)
    for tile in range(S):
        at = tile * (CB + 1)
        out_ref[:, tile * LANES : (tile + 1) * LANES] = turned[at : at + CB, :]


def correlate(got, scale):
    _, n_stn, n_time, channels, _ = got.shape
    return pl.pallas_call(
        lambda *refs: correlate_kernel(scale, *refs),
        out_shape=jax.ShapeDtypeStruct((channels, 2 * S * S), jnp.float32),
        grid=(channels // CB,),
        in_specs=[pl.BlockSpec((2, n_stn, n_time, CB, LANES), lambda i: (0, 0, 0, i, 0))],
        out_specs=pl.BlockSpec((CB, 2 * S * S), lambda i: (i, 0)),
        scratch_shapes=[
            pltpu.VMEM((CB * (4 * n_time + 1), LANES), jnp.float32),
            pltpu.VMEM((8 * S, LANES), jnp.float32),
            pltpu.VMEM((S * (CB + 1), LANES), jnp.float32),
        ],
        compiler_params=pltpu.CompilerParams(vmem_limit_bytes=VMEM_LIMIT),
        cost_estimate=pl.CostEstimate(
            flops=2 * channels * 64 * 128 * 128, bytes_accessed=26 * 2**20, transcendentals=0
        ),
    )(got)


def fast_shards(samples, delays, valid, tone_chan):
    tables = fast_tables()
    sizes = tuple(lax.axis_size(name) for name in ("stn", "tm", "cores"))
    n_stn, n_tm, n_cores = sizes
    stations, stretch = samples.shape
    trailing = passed_along(samples[:, :MAXD], ("tm", "cores"), -1)
    blocks = samples.reshape(stations, stretch // LANES, LANES)
    zero = channelize_pair(0, blocks, (blocks, 2), delays, valid, tables)
    halo = trailing.reshape(stations, MAXD // LANES, LANES)
    channels = NCH // math.prod(sizes)
    scale = 1.0 / math.sqrt(stretch // (FA * FB) * n_tm * n_cores)
    got, picks = exchange(zero, blocks, halo, delays, valid, tone_chan, tables, sizes, scale)
    got = got.reshape(2, n_stn, n_tm * n_cores, channels, LANES)
    visibility = correlate(got, scale)
    mine = picks.reshape(NTONE, 2, 2, stations)[:, :, 0]
    phase_cal = jnp.transpose(mine, (2, 1, 0)).reshape(stations, 2 * NTONE)
    return (visibility, phase_cal)


def solution(mesh):
    sizes = mesh.shape
    body = fast_shards if sizes["stn"] == 2 and math.prod(sizes.values()) == 32 else shards
    return jax.shard_map(
        body,
        mesh=mesh,
        in_specs=(P("stn", ("tm", "cores")), P("stn"), P("stn"), P("stn", None)),
        out_specs=(P(("stn", "tm", "cores"), None), P("stn", None)),
        check_vma=False,
    )
```

```python
import math

import jax
import jax.numpy as jnp
import ml_dtypes
import numpy as np
from jax import lax
from jax.experimental import pallas as pl
from jax.experimental.pallas import tpu as pltpu
from jax.sharding import PartitionSpec as P

S = 64
NCH = 16384
FA = 256
FB = 128
NTONE = 64
MAXD = 32768


def passed_along(block, axis, distance):
    devices = range(lax.axis_size(axis))
    route = [(i - distance, i) for i in devices if i - distance in devices]
    return lax.ppermute(block, axis, route)


def make_tables():
    outer_idx = jnp.arange(FA, dtype=jnp.int32)
    phases = outer_idx[:, None] * outer_idx[None, :] % FA
    angles = 2.0 * math.pi / FA * phases.astype(jnp.float32)
    section_one = jnp.stack([jnp.cos(angles), -jnp.sin(angles)]).astype(jnp.bfloat16)
    inner_idx = jnp.arange(FB, dtype=jnp.int32)
    spectrum_len = FA * FB
    twist_idx = outer_idx[:, None] * inner_idx[None, :] % spectrum_len
    twists = 2.0 * math.pi / spectrum_len * twist_idx.astype(jnp.float32)
    norm_scale = 1.0 / math.sqrt(spectrum_len)
    twist_cos = jnp.cos(twists) * norm_scale
    twist_sin = jnp.sin(twists) * norm_scale
    half_idx = jnp.arange(FB // 2, dtype=jnp.int32)
    last_idx = inner_idx[:, None] * half_idx[None, :] % FB
    thetas = 2.0 * math.pi / FB * last_idx.astype(jnp.float32)
    cosine = jnp.cos(thetas)
    sine_val = jnp.sin(thetas)
    section_two = jnp.stack(
        [jnp.stack([cosine, -sine_val], axis=1), jnp.stack([sine_val, cosine], axis=1)]
    ).astype(jnp.bfloat16)
    return (section_one, twist_cos, twist_sin, section_two)


def channelize(window, usable, tables):
    section_one, twist_cos, twist_sin, section_two = tables
    spec_count = window.shape[0] // (FA * FB)
    blocks = window.reshape(spec_count, FA, FB)
    section_out = jnp.einsum(
        "xkn,bnm->bxkm", section_one, blocks, preferred_element_type=jnp.float32
    )
    real_part = section_out[:, 0] * twist_cos + section_out[:, 1] * twist_sin
    imag_part = section_out[:, 1] * twist_cos - section_out[:, 0] * twist_sin
    twisted = jnp.stack([real_part, imag_part], axis=1).astype(jnp.bfloat16)
    product = jnp.einsum(
        "xnrq,bxkn->brqk", section_two, twisted, preferred_element_type=jnp.float32
    )
    return (product.reshape(spec_count, 2, NCH) * usable).astype(jnp.bfloat16)


def cross_power(matrix):
    gram = jnp.einsum("cta,ctb->cab", matrix, matrix, preferred_element_type=jnp.float32)
    real_re = gram[:, :S, :S]
    imag_im = gram[:, S:, S:]
    imag_re = gram[:, S:, :S]
    real_im = gram[:, :S, S:]
    channels = gram.shape[0]
    first = (real_re + imag_im).reshape(channels, S * S)
    second = (imag_re - real_im).reshape(channels, S * S)
    return jnp.concatenate([first, second], axis=1)


def shards(samples, delays, valid, tone_chan):
    tables = make_tables()
    stretch = samples.shape[1]
    spectrum_len = FA * FB
    trailing = passed_along(samples[:, :MAXD], ("tm", "cores"), -1)
    extended = jnp.concatenate([samples, trailing], axis=1)
    chan_ids = jnp.arange(NCH, dtype=jnp.int32)

    def station(inputs):
        stream, shift_by, usable, tone_ids = inputs
        window = lax.dynamic_slice_in_dim(stream, shift_by, stretch)
        spectra = channelize(window, usable.astype(jnp.float32), tables)
        totals = jnp.sum(spectra, axis=0, dtype=jnp.float32)
        selector = (chan_ids[:, None] == tone_ids[None, :]).astype(jnp.float32)
        picked = jnp.dot(
            totals, selector, precision=lax.Precision.HIGHEST, preferred_element_type=jnp.float32
        )
        return (spectra, picked.reshape(2 * NTONE))

    spectra, tone_picks = lax.map(station, (extended, delays, valid, tone_chan))
    spectra_all = stretch // spectrum_len * lax.axis_size("tm") * lax.axis_size("cores")
    norm_scale = 1.0 / math.sqrt(spectra_all)
    phase_cal = lax.psum(tone_picks, ("tm", "cores")) * norm_scale
    local_stn = spectra.shape[0]
    spec_here = spectra.shape[1]
    n_stn = lax.axis_size("stn")
    n_tm = lax.axis_size("tm")
    received = lax.all_to_all(spectra[None], ("stn", "tm"), split_axis=4, concat_axis=0, tiled=True)
    block_in = received.shape[4]
    arranged = received.reshape(n_stn, n_tm, local_stn, spec_here, 2, block_in)
    turned = jnp.transpose(arranged, (0, 2, 1, 3, 4, 5)).reshape(
        n_stn * local_stn, n_tm * spec_here, 2, block_in
    )
    block = turned.shape[3]
    halves = turned.reshape(turned.shape[0], turned.shape[1], 2, 2, block // 2)
    halves = lax.all_to_all(halves, "cores", split_axis=3, concat_axis=1, tiled=True)
    turned = halves.reshape(halves.shape[0], halves.shape[1], 2, block // 2)
    rows = turned.shape[1]
    matrix = jnp.transpose(turned, (3, 1, 2, 0)).reshape(turned.shape[3], rows, 2 * S)
    partial_value = cross_power(matrix)
    return (partial_value * norm_scale, phase_cal)


LANES = 128
VMEM_LIMIT = 56 * 1024 * 1024


def fast_tables():
    def turn(left, right, period):
        angle = np.float32(2.0 * math.pi / period)
        phases = (np.arange(left)[:, None] * np.arange(right)[None, :] % period).astype(np.float32)
        return np.cos(angle * phases), np.sin(angle * phases)

    cosine, sine = turn(FA, FA, FA)
    first = np.concatenate([cosine, -sine], axis=0).astype(ml_dtypes.bfloat16)
    cosine, sine = turn(FA, FB, FA * FB)
    norm_scale = np.float32(1.0 / math.sqrt(FA * FB))
    twist_cos, twist_sin = cosine * norm_scale, sine * norm_scale
    cosine, sine = turn(FB // 2, FB, FB)
    last = np.concatenate([cosine, sine], axis=1).astype(ml_dtypes.bfloat16)
    return tuple(jnp.asarray(table) for table in (first, twist_cos, twist_sin, last))


def first_stage(s, delay, usable, one_ref, cos_ref, sin_ref, stream, twist_re, twist_im):
    rows = 2 * FA
    whole = delay // LANES
    part = delay % LANES
    lane = lax.broadcasted_iota(jnp.int32, (rows, LANES), 1)
    here = stream[pl.ds(whole, rows), :]
    after = stream[pl.ds(whole + 1, rows), :]
    mixed = jnp.where(lane < part, after, here)
    shifted = pltpu.roll(mixed, (LANES - part) % LANES, 1).astype(jnp.bfloat16)
    both = jnp.concatenate([shifted[:FA], shifted[FA:]], axis=1)
    section = jnp.dot(one_ref[...], both, preferred_element_type=jnp.float32)
    cosine = cos_ref[...] * usable
    sine = sin_ref[...] * usable
    for t in range(2):
        re = section[:FA, t * LANES : (t + 1) * LANES]
        im = section[FA:, t * LANES : (t + 1) * LANES]
        twist_re[pl.ds(t * 32 + s, FA, stride=PITCH), :] = re * cosine + im * sine
        twist_im[pl.ds(t * 32 + s, FA, stride=PITCH), :] = im * cosine - re * sine


def second_stage(two_ref, out_ref, twist_re, twist_im, turned):
    def second(k, carry):
        re = twist_re[pl.ds(k * PITCH, 64), :].astype(jnp.bfloat16)
        im = twist_im[pl.ds(k * PITCH, 64), :].astype(jnp.bfloat16)
        right = jnp.concatenate(
            [jnp.concatenate([re, im], axis=1), jnp.concatenate([im, -re], axis=1)], axis=0
        )
        product = lax.dot_general(
            two_ref[...], right, (((1,), (1,)), ((), ())), preferred_element_type=jnp.float32
        )
        turned[pl.ds(k, FB // 2, stride=FA + 1), :] = product
        return carry

    lax.fori_loop(0, FA, second, 0, unroll=8)

    def write(q, carry):
        out_ref[q] = turned[pl.ds(q * (FA + 1), FA), :].astype(jnp.bfloat16)
        return carry

    lax.fori_loop(0, FB // 2, write, 0, unroll=2)


PITCH = 65
STAGE_SCRATCH = [
    pltpu.VMEM((3 * FA + 8, LANES), jnp.float32),
    pltpu.VMEM((FA * PITCH + 7, LANES), jnp.float32),
    pltpu.VMEM((FA * PITCH + 7, LANES), jnp.float32),
    pltpu.VMEM(((FA + 1) * FB // 2, LANES), jnp.float32),
]


def channelize_kernel(delay_ref, valid_ref, main_ref, next_ref, one_ref, cos_ref, sin_ref, two_ref,
                      out_ref, stream, twist_re, twist_im, turned):
    s = pl.program_id(0)
    rows = 2 * FA
    stream[0:rows, :] = main_ref[0].astype(jnp.float32)
    stream[rows : rows + FA, :] = next_ref[0].astype(jnp.float32)
    first_stage(s, delay_ref[s], valid_ref[s].astype(jnp.float32), one_ref, cos_ref, sin_ref,
                stream, twist_re, twist_im)

    @pl.when(s == pl.num_programs(0) - 1)
    def _():
        second_stage(two_ref, out_ref, twist_re, twist_im, turned)


def channelize_pair(pair, blocks, following, delays, valid, tables):
    first, twist_cos, twist_sin, last = tables
    source, next_at = following
    whole = lambda shape: pl.BlockSpec(shape, lambda s, *_: (0,) * len(shape))
    return pl.pallas_call(
        channelize_kernel,
        out_shape=jax.ShapeDtypeStruct((FB // 2, FA, LANES), jnp.bfloat16),
        grid_spec=pltpu.PrefetchScalarGridSpec(
            num_scalar_prefetch=2,
            grid=(blocks.shape[0],),
            in_specs=[
                pl.BlockSpec((1, 2 * FA, LANES), lambda s, *_: (s, pair, 0)),
                pl.BlockSpec((1, FA, LANES), lambda s, *_: (s, next_at, 0)),
                whole((2 * FA, FA)),
                whole((FA, FB)),
                whole((FA, FB)),
                whole((FB // 2, 2 * FB)),
            ],
            out_specs=whole((FB // 2, FA, LANES)),
            scratch_shapes=STAGE_SCRATCH,
        ),
        compiler_params=pltpu.CompilerParams(vmem_limit_bytes=VMEM_LIMIT),
        cost_estimate=pl.CostEstimate(
            flops=3 * 2 * 64 * 256 * 256 * 256, bytes_accessed=10 * 2**20, transcendentals=0
        ),
    )(delays, valid, blocks, source, first, twist_cos, twist_sin, last)


def linear_index(sizes):
    n_stn, n_tm, n_cores = sizes
    return (lax.axis_index("stn") * n_tm + lax.axis_index("tm")) * n_cores + lax.axis_index("cores")


def pick_tones(tone_ref, turned, picks, stations, first):
    lane = lax.broadcasted_iota(jnp.int32, (1, LANES), 1) % 32

    def tone(k, carry):
        row = jnp.zeros((1, LANES), jnp.float32)
        for s in range(stations):
            channel = tone_ref[s, k]
            row = jnp.where(lane == s, turned[pl.ds(channel + channel // FA, 1), :], row)
        row = row.astype(jnp.bfloat16).astype(jnp.float32)
        picks[pl.ds(k, 1), :] = row if first else picks[pl.ds(k, 1), :] + row
        return carry

    lax.fori_loop(0, NTONE, tone, 0)


def exchange_kernel(sizes, scale, zero_ref, delay_ref, valid_ref, tone_ref, blocks_ref, halo_ref, one_ref,
                    cos_ref, sin_ref, two_ref, got_ref, tones_ref, stream, twist_re, twist_im,
                    turned, later, main_ref, next_ref, picks, sent, arrived, local_sem, send_sem, recv_sem, load_sem,
                    tone_send, tone_recv):
    _, n_tm, n_cores = sizes
    n = math.prod(sizes)
    me = linear_index(sizes)

    self_at = 4

    def place(i):
        turn = (i + i // n_tm) % 4
        return (
            (lax.axis_index("stn") + turn // 2) % 2,
            (lax.axis_index("tm") + 3 * i + 4) % n_tm,
            (lax.axis_index("cores") + turn) % 2,
        )

    def others(body):
        def step(i, carry):
            body(i)
            return carry

        lax.fori_loop(0, self_at, step, 0)
        lax.fori_loop(self_at + 1, n, step, 0)

    barrier = pltpu.get_barrier_semaphore()

    others(
        lambda i: pl.semaphore_signal(
            barrier, inc=1, device_id=place(i), device_id_type=pl.DeviceIdType.MESH
        )
    )
    pl.semaphore_wait(barrier, n - 1)
    sources = (zero_ref, later)

    def copy(pair, k):
        where = place(k)
        to = (where[0] * n_tm + where[1]) * n_cores + where[2]
        return pltpu.make_async_remote_copy(
            src_ref=sources[pair].at[pl.ds(to * 2, 2)],
            dst_ref=got_ref.at[pair, me],
            send_sem=send_sem.at[pair, k],
            recv_sem=recv_sem.at[pair, k],
            device_id=where,
            device_id_type=pl.DeviceIdType.MESH,
        )

    def own(pair):
        return pltpu.make_async_copy(
            sources[pair].at[pl.ds(me * 2, 2)], got_ref.at[pair, me], local_sem.at[pair]
        )

    def send(pair):
        others(lambda i: copy(pair, i).start())
        own(pair).start()

    def finish(pair):
        own(pair).wait()
        others(lambda i: copy(pair, i).wait())

    send(0)
    loads = [
        pltpu.make_async_copy(zero_ref, later, load_sem.at[0]),
        pltpu.make_async_copy(blocks_ref.at[:, pl.ds(2 * FA, 2 * FA)], main_ref, load_sem.at[1]),
        pltpu.make_async_copy(halo_ref, next_ref, load_sem.at[2]),
    ]
    for load in loads:
        load.start()
    loads[0].wait()

    def widen(q, carry):
        turned[pl.ds(q * (FA + 1), FA), :] = later[q].astype(jnp.float32)
        return carry

    lax.fori_loop(0, FB // 2, widen, 0, unroll=2)
    stations = main_ref.shape[0]
    pick_tones(tone_ref, turned, picks, stations, True)

    def station(s, carry):
        rows = 2 * FA
        stream[0:rows, :] = main_ref[s].astype(jnp.float32)
        stream[rows : rows + FA, :] = next_ref[s].astype(jnp.float32)
        first_stage(s, delay_ref[s], valid_ref[s].astype(jnp.float32), one_ref, cos_ref, sin_ref,
                    stream, twist_re, twist_im)
        return carry

    loads[1].wait()
    loads[2].wait()
    lax.fori_loop(0, stations, station, 0)
    second_stage(two_ref, later, twist_re, twist_im, turned)
    send(1)
    pick_tones(tone_ref, turned, picks, stations, False)
    running = picks[...] + pltpu.roll(picks[...], 96, 1)
    flips = []
    for name, size in (("cores", n_cores), ("tm", n_tm)):
        bit = 1
        while bit < size:
            at = lax.axis_index(name)
            flips.append({name: at + bit * (1 - 2 * ((at // bit) % 2))})
            bit *= 2
    for r, partner in enumerate(flips):
        sent[r] = running
        passing = pltpu.make_async_remote_copy(
            src_ref=sent.at[r],
            dst_ref=arrived.at[r],
            send_sem=tone_send.at[r],
            recv_sem=tone_recv.at[r],
            device_id=partner,
            device_id_type=pl.DeviceIdType.MESH,
        )
        passing.start()
        passing.wait()
        running = running + arrived[r]
    tones_ref[...] = running * scale
    finish(0)
    finish(1)


def exchange(zero, blocks, halo, delays, valid, tone_chan, tables, sizes, scale):
    n = math.prod(sizes)
    rounds = (sizes[1] * sizes[2]).bit_length() - 1
    stations = blocks.shape[0]
    whole = lambda shape: pl.BlockSpec(shape, lambda i: (0,) * len(shape))
    smem = pl.BlockSpec(memory_space=pltpu.SMEM)
    return pl.pallas_call(
        lambda *refs: exchange_kernel(sizes, scale, *refs),
        out_shape=(
            jax.ShapeDtypeStruct((2, n, 2, FA, LANES), jnp.bfloat16),
            jax.ShapeDtypeStruct((NTONE, LANES), jnp.float32),
        ),
        grid=(1,),
        in_specs=[
            pl.BlockSpec(memory_space=pl.ANY),
            smem,
            smem,
            smem,
            pl.BlockSpec(memory_space=pl.ANY),
            pl.BlockSpec(memory_space=pl.ANY),
            whole((2 * FA, FA)),
            whole((FA, FB)),
            whole((FA, FB)),
            whole((FB // 2, 2 * FB)),
        ],
        out_specs=(pl.BlockSpec(memory_space=pl.ANY), whole((NTONE, LANES))),
        scratch_shapes=STAGE_SCRATCH
        + [
            pltpu.VMEM((FB // 2, FA, LANES), jnp.bfloat16),
            pltpu.VMEM((stations, 2 * FA, LANES), jnp.bfloat16),
            pltpu.VMEM((stations, FA, LANES), jnp.bfloat16),
            pltpu.VMEM((NTONE, LANES), jnp.float32),
            pltpu.VMEM((rounds, NTONE, LANES), jnp.float32),
            pltpu.VMEM((rounds, NTONE, LANES), jnp.float32),
            pltpu.SemaphoreType.DMA((2,)),
            pltpu.SemaphoreType.DMA((2, n)),
            pltpu.SemaphoreType.DMA((2, n)),
            pltpu.SemaphoreType.DMA((3,)),
            pltpu.SemaphoreType.DMA((rounds,)),
            pltpu.SemaphoreType.DMA((rounds,)),
        ],
        compiler_params=pltpu.CompilerParams(
            collective_id=0, has_side_effects=True, vmem_limit_bytes=VMEM_LIMIT
        ),
    )(zero, delays, valid, tone_chan, blocks, halo, *tables)


CB = 64


def correlate_kernel(scale, got_ref, out_ref, matrix, power, turned):
    lane = lax.broadcasted_iota(jnp.int32, (CB, LANES), 1)
    low = lane % 64 < 32
    n_time = got_ref.shape[2]
    rows = 4 * n_time
    pitch = rows + 1
    for u in range(2):
        for j in range(n_time):
            y0 = got_ref[u, 0, j].astype(jnp.float32)
            y1 = got_ref[u, 1, j].astype(jnp.float32)
            t = (u * n_time + j) * 2
            matrix[pl.ds(t, CB, stride=pitch), :] = jnp.where(low, y0, pltpu.roll(y1, 32, 1))
            matrix[pl.ds(t + 1, CB, stride=pitch), :] = jnp.where(low, pltpu.roll(y0, 96, 1), y1)
    left = lax.broadcasted_iota(jnp.int32, (S, LANES), 1) < 64
    left_half = lax.broadcasted_iota(jnp.int32, (S // 2, LANES), 1) < 64

    def channel(c, carry):
        values = matrix[pl.ds(c * pitch, rows), :].astype(jnp.bfloat16)
        gram = lax.dot_general(
            values, values, (((0,), (0,)), ((), ())), preferred_element_type=jnp.float32
        )
        upper = gram[:S] * scale
        lower = pltpu.roll(gram[S:] * scale, 64, 1)
        slot = pl.multiple_of((c % 8) * S, S)
        power[pl.ds(slot, S), :] = jnp.where(left, upper + lower, lower - upper)
        even = power[pl.ds(slot, S // 2, stride=2), :]
        odd = power[pl.ds(slot + 1, S // 2, stride=2), :]
        turned[pl.ds(c, S // 2, stride=CB + 1), :] = jnp.where(left_half, even, pltpu.roll(odd, 64, 1))
        turned[pl.ds(S // 2 * (CB + 1) + c, S // 2, stride=CB + 1), :] = jnp.where(
            left_half, pltpu.roll(even, 64, 1), odd
        )
        return carry

    lax.fori_loop(0, CB, channel, 0, unroll=8)
    for tile in range(S):
        at = tile * (CB + 1)
        out_ref[:, tile * LANES : (tile + 1) * LANES] = turned[at : at + CB, :]


def correlate(got, scale):
    _, n_stn, n_time, channels, _ = got.shape
    return pl.pallas_call(
        lambda *refs: correlate_kernel(scale, *refs),
        out_shape=jax.ShapeDtypeStruct((channels, 2 * S * S), jnp.float32),
        grid=(channels // CB,),
        in_specs=[pl.BlockSpec((2, n_stn, n_time, CB, LANES), lambda i: (0, 0, 0, i, 0))],
        out_specs=pl.BlockSpec((CB, 2 * S * S), lambda i: (i, 0)),
        scratch_shapes=[
            pltpu.VMEM((CB * (4 * n_time + 1), LANES), jnp.float32),
            pltpu.VMEM((8 * S, LANES), jnp.float32),
            pltpu.VMEM((S * (CB + 1), LANES), jnp.float32),
        ],
        compiler_params=pltpu.CompilerParams(vmem_limit_bytes=VMEM_LIMIT),
        cost_estimate=pl.CostEstimate(
            flops=2 * channels * 64 * 128 * 128, bytes_accessed=26 * 2**20, transcendentals=0
        ),
    )(got)


def fast_shards(samples, delays, valid, tone_chan):
    tables = fast_tables()
    sizes = tuple(lax.axis_size(name) for name in ("stn", "tm", "cores"))
    n_stn, n_tm, n_cores = sizes
    stations, stretch = samples.shape
    trailing = passed_along(samples[:, :MAXD], ("tm", "cores"), -1)
    blocks = samples.reshape(stations, stretch // LANES, LANES)
    zero = channelize_pair(0, blocks, (blocks, 2), delays, valid, tables)
    halo = trailing.reshape(stations, MAXD // LANES, LANES)
    channels = NCH // math.prod(sizes)
    scale = 1.0 / math.sqrt(stretch // (FA * FB) * n_tm * n_cores)
    got, picks = exchange(zero, blocks, halo, delays, valid, tone_chan, tables, sizes, scale)
    got = got.reshape(2, n_stn, n_tm * n_cores, channels, LANES)
    visibility = correlate(got, scale)
    mine = picks.reshape(NTONE, 2, 2, stations)[:, :, 0]
    phase_cal = jnp.transpose(mine, (2, 1, 0)).reshape(stations, 2 * NTONE)
    return (visibility, phase_cal)


def solution(mesh):
    sizes = mesh.shape
    body = fast_shards if sizes["stn"] == 2 and math.prod(sizes.values()) == 32 else shards
    return jax.shard_map(
        body,
        mesh=mesh,
        in_specs=(P("stn", ("tm", "cores")), P("stn"), P("stn"), P("stn", None)),
        out_specs=(P(("stn", "tm", "cores"), None), P("stn", None)),
        check_vma=False,
    )
```

```python
import math

import jax
import jax.numpy as jnp
import ml_dtypes
import numpy as np
from jax import lax
from jax.experimental import pallas as pl
from jax.experimental.pallas import tpu as pltpu
from jax.sharding import PartitionSpec as P

S = 64
NCH = 16384
FA = 256
FB = 128
NTONE = 64
MAXD = 32768


def passed_along(block, axis, distance):
    devices = range(lax.axis_size(axis))
    route = [(i - distance, i) for i in devices if i - distance in devices]
    return lax.ppermute(block, axis, route)


def make_tables():
    outer_idx = jnp.arange(FA, dtype=jnp.int32)
    phases = outer_idx[:, None] * outer_idx[None, :] % FA
    angles = 2.0 * math.pi / FA * phases.astype(jnp.float32)
    section_one = jnp.stack([jnp.cos(angles), -jnp.sin(angles)]).astype(jnp.bfloat16)
    inner_idx = jnp.arange(FB, dtype=jnp.int32)
    spectrum_len = FA * FB
    twist_idx = outer_idx[:, None] * inner_idx[None, :] % spectrum_len
    twists = 2.0 * math.pi / spectrum_len * twist_idx.astype(jnp.float32)
    norm_scale = 1.0 / math.sqrt(spectrum_len)
    twist_cos = jnp.cos(twists) * norm_scale
    twist_sin = jnp.sin(twists) * norm_scale
    half_idx = jnp.arange(FB // 2, dtype=jnp.int32)
    last_idx = inner_idx[:, None] * half_idx[None, :] % FB
    thetas = 2.0 * math.pi / FB * last_idx.astype(jnp.float32)
    cosine = jnp.cos(thetas)
    sine_val = jnp.sin(thetas)
    section_two = jnp.stack(
        [jnp.stack([cosine, -sine_val], axis=1), jnp.stack([sine_val, cosine], axis=1)]
    ).astype(jnp.bfloat16)
    return (section_one, twist_cos, twist_sin, section_two)


def channelize(window, usable, tables):
    section_one, twist_cos, twist_sin, section_two = tables
    spec_count = window.shape[0] // (FA * FB)
    blocks = window.reshape(spec_count, FA, FB)
    section_out = jnp.einsum(
        "xkn,bnm->bxkm", section_one, blocks, preferred_element_type=jnp.float32
    )
    real_part = section_out[:, 0] * twist_cos + section_out[:, 1] * twist_sin
    imag_part = section_out[:, 1] * twist_cos - section_out[:, 0] * twist_sin
    twisted = jnp.stack([real_part, imag_part], axis=1).astype(jnp.bfloat16)
    product = jnp.einsum(
        "xnrq,bxkn->brqk", section_two, twisted, preferred_element_type=jnp.float32
    )
    return (product.reshape(spec_count, 2, NCH) * usable).astype(jnp.bfloat16)


def cross_power(matrix):
    gram = jnp.einsum("cta,ctb->cab", matrix, matrix, preferred_element_type=jnp.float32)
    real_re = gram[:, :S, :S]
    imag_im = gram[:, S:, S:]
    imag_re = gram[:, S:, :S]
    real_im = gram[:, :S, S:]
    channels = gram.shape[0]
    first = (real_re + imag_im).reshape(channels, S * S)
    second = (imag_re - real_im).reshape(channels, S * S)
    return jnp.concatenate([first, second], axis=1)


def shards(samples, delays, valid, tone_chan):
    tables = make_tables()
    stretch = samples.shape[1]
    spectrum_len = FA * FB
    trailing = passed_along(samples[:, :MAXD], ("tm", "cores"), -1)
    extended = jnp.concatenate([samples, trailing], axis=1)
    chan_ids = jnp.arange(NCH, dtype=jnp.int32)

    def station(inputs):
        stream, shift_by, usable, tone_ids = inputs
        window = lax.dynamic_slice_in_dim(stream, shift_by, stretch)
        spectra = channelize(window, usable.astype(jnp.float32), tables)
        totals = jnp.sum(spectra, axis=0, dtype=jnp.float32)
        selector = (chan_ids[:, None] == tone_ids[None, :]).astype(jnp.float32)
        picked = jnp.dot(
            totals, selector, precision=lax.Precision.HIGHEST, preferred_element_type=jnp.float32
        )
        return (spectra, picked.reshape(2 * NTONE))

    spectra, tone_picks = lax.map(station, (extended, delays, valid, tone_chan))
    spectra_all = stretch // spectrum_len * lax.axis_size("tm") * lax.axis_size("cores")
    norm_scale = 1.0 / math.sqrt(spectra_all)
    phase_cal = lax.psum(tone_picks, ("tm", "cores")) * norm_scale
    local_stn = spectra.shape[0]
    spec_here = spectra.shape[1]
    n_stn = lax.axis_size("stn")
    n_tm = lax.axis_size("tm")
    received = lax.all_to_all(spectra[None], ("stn", "tm"), split_axis=4, concat_axis=0, tiled=True)
    block_in = received.shape[4]
    arranged = received.reshape(n_stn, n_tm, local_stn, spec_here, 2, block_in)
    turned = jnp.transpose(arranged, (0, 2, 1, 3, 4, 5)).reshape(
        n_stn * local_stn, n_tm * spec_here, 2, block_in
    )
    block = turned.shape[3]
    halves = turned.reshape(turned.shape[0], turned.shape[1], 2, 2, block // 2)
    halves = lax.all_to_all(halves, "cores", split_axis=3, concat_axis=1, tiled=True)
    turned = halves.reshape(halves.shape[0], halves.shape[1], 2, block // 2)
    rows = turned.shape[1]
    matrix = jnp.transpose(turned, (3, 1, 2, 0)).reshape(turned.shape[3], rows, 2 * S)
    partial_value = cross_power(matrix)
    return (partial_value * norm_scale, phase_cal)


LANES = 128
VMEM_LIMIT = 56 * 1024 * 1024


def fast_tables():
    def turn(left, right, period):
        angle = np.float32(2.0 * math.pi / period)
        phases = (np.arange(left)[:, None] * np.arange(right)[None, :] % period).astype(np.float32)
        return np.cos(angle * phases), np.sin(angle * phases)

    cosine, sine = turn(FA, FA, FA)
    first = np.concatenate([cosine, -sine], axis=0).astype(ml_dtypes.bfloat16)
    cosine, sine = turn(FA, FB, FA * FB)
    norm_scale = np.float32(1.0 / math.sqrt(FA * FB))
    twist_cos, twist_sin = cosine * norm_scale, sine * norm_scale
    cosine, sine = turn(FB // 2, FB, FB)
    last = np.concatenate([cosine, sine], axis=1).astype(ml_dtypes.bfloat16)
    return tuple(jnp.asarray(table) for table in (first, twist_cos, twist_sin, last))


def first_stage(s, delay, usable, one_ref, cos_ref, sin_ref, stream, twist_re, twist_im):
    rows = 2 * FA
    whole = delay // LANES
    part = delay % LANES
    lane = lax.broadcasted_iota(jnp.int32, (rows, LANES), 1)
    here = stream[pl.ds(whole, rows), :]
    after = stream[pl.ds(whole + 1, rows), :]
    mixed = jnp.where(lane < part, after, here)
    shifted = pltpu.roll(mixed, (LANES - part) % LANES, 1).astype(jnp.bfloat16)
    both = jnp.concatenate([shifted[:FA], shifted[FA:]], axis=1)
    section = jnp.dot(one_ref[...], both, preferred_element_type=jnp.float32)
    cosine = cos_ref[...] * usable
    sine = sin_ref[...] * usable
    for t in range(2):
        re = section[:FA, t * LANES : (t + 1) * LANES]
        im = section[FA:, t * LANES : (t + 1) * LANES]
        twist_re[pl.ds(t * 32 + s, FA, stride=PITCH), :] = re * cosine + im * sine
        twist_im[pl.ds(t * 32 + s, FA, stride=PITCH), :] = im * cosine - re * sine


def second_stage(two_ref, out_ref, twist_re, twist_im, turned):
    def second(k, carry):
        re = twist_re[pl.ds(k * PITCH, 64), :].astype(jnp.bfloat16)
        im = twist_im[pl.ds(k * PITCH, 64), :].astype(jnp.bfloat16)
        right = jnp.concatenate(
            [jnp.concatenate([re, im], axis=1), jnp.concatenate([im, -re], axis=1)], axis=0
        )
        product = lax.dot_general(
            two_ref[...], right, (((1,), (1,)), ((), ())), preferred_element_type=jnp.float32
        )
        turned[pl.ds(k, FB // 2, stride=FA + 1), :] = product
        return carry

    lax.fori_loop(0, FA, second, 0, unroll=16)

    def write(q, carry):
        out_ref[q] = turned[pl.ds(q * (FA + 1), FA), :].astype(jnp.bfloat16)
        return carry

    lax.fori_loop(0, FB // 2, write, 0, unroll=2)


PITCH = 65
TOGETHER = 4
STAGE_SCRATCH = [
    pltpu.VMEM((3 * FA + 8, LANES), jnp.float32),
    pltpu.VMEM((FA * PITCH + 7, LANES), jnp.float32),
    pltpu.VMEM((FA * PITCH + 7, LANES), jnp.float32),
    pltpu.VMEM(((FA + 1) * FB // 2, LANES), jnp.float32),
]


def channelize_kernel(delay_ref, valid_ref, main_ref, next_ref, one_ref, cos_ref, sin_ref, two_ref,
                      out_ref, stream, twist_re, twist_im, turned):
    rows = 2 * FA
    for i in range(TOGETHER):
        stream[i, 0:rows, :] = main_ref[i].astype(jnp.float32)
        stream[i, rows : rows + FA, :] = next_ref[i].astype(jnp.float32)
    for i in range(TOGETHER):
        s = pl.program_id(0) * TOGETHER + i
        first_stage(s, delay_ref[s], valid_ref[s].astype(jnp.float32), one_ref, cos_ref, sin_ref,
                    stream.at[i], twist_re, twist_im)

    @pl.when(pl.program_id(0) == pl.num_programs(0) - 1)
    def _():
        second_stage(two_ref, out_ref, twist_re, twist_im, turned)


def channelize_pair(pair, blocks, following, delays, valid, tables):
    first, twist_cos, twist_sin, last = tables
    source, next_at = following
    whole = lambda shape: pl.BlockSpec(shape, lambda s, *_: (0,) * len(shape))
    return pl.pallas_call(
        channelize_kernel,
        out_shape=jax.ShapeDtypeStruct((FB // 2, FA, LANES), jnp.bfloat16),
        grid_spec=pltpu.PrefetchScalarGridSpec(
            num_scalar_prefetch=2,
            grid=(blocks.shape[0] // TOGETHER,),
            in_specs=[
                pl.BlockSpec((TOGETHER, 2 * FA, LANES), lambda s, *_: (s, pair, 0)),
                pl.BlockSpec((TOGETHER, FA, LANES), lambda s, *_: (s, next_at, 0)),
                whole((2 * FA, FA)),
                whole((FA, FB)),
                whole((FA, FB)),
                whole((FB // 2, 2 * FB)),
            ],
            out_specs=whole((FB // 2, FA, LANES)),
            scratch_shapes=[pltpu.VMEM((TOGETHER, 3 * FA + 8, LANES), jnp.float32)] + STAGE_SCRATCH[1:],
        ),
        compiler_params=pltpu.CompilerParams(vmem_limit_bytes=VMEM_LIMIT),
        cost_estimate=pl.CostEstimate(
            flops=3 * 2 * 64 * 256 * 256 * 256, bytes_accessed=10 * 2**20, transcendentals=0
        ),
    )(delays, valid, blocks, source, first, twist_cos, twist_sin, last)


def linear_index(sizes):
    n_stn, n_tm, n_cores = sizes
    return (lax.axis_index("stn") * n_tm + lax.axis_index("tm")) * n_cores + lax.axis_index("cores")


def pick_tones(tone_ref, turned, picks, stations, first):
    lane = lax.broadcasted_iota(jnp.int32, (1, LANES), 1) % 32

    def tone(k, carry):
        row = jnp.zeros((1, LANES), jnp.float32)
        for s in range(stations):
            channel = tone_ref[s, k]
            row = jnp.where(lane == s, turned[pl.ds(channel + channel // FA, 1), :], row)
        row = row.astype(jnp.bfloat16).astype(jnp.float32)
        picks[pl.ds(k, 1), :] = row if first else picks[pl.ds(k, 1), :] + row
        return carry

    lax.fori_loop(0, NTONE, tone, 0)


def exchange_kernel(sizes, scale, zero_ref, delay_ref, valid_ref, tone_ref, blocks_ref, halo_ref, one_ref,
                    cos_ref, sin_ref, two_ref, got_ref, tones_ref, stream, twist_re, twist_im,
                    turned, later, main_ref, next_ref, picks, sent, arrived, local_sem, send_sem, recv_sem, load_sem,
                    tone_send, tone_recv):
    _, n_tm, n_cores = sizes
    n = math.prod(sizes)
    me = linear_index(sizes)

    self_at = 4

    def place(i):
        turn = (i + i // n_tm) % 4
        return (
            (lax.axis_index("stn") + turn // 2) % 2,
            (lax.axis_index("tm") + 3 * i + 4) % n_tm,
            (lax.axis_index("cores") + turn) % 2,
        )

    def others(body):
        def step(i, carry):
            body(i)
            return carry

        lax.fori_loop(0, self_at, step, 0)
        lax.fori_loop(self_at + 1, n, step, 0)

    barrier = pltpu.get_barrier_semaphore()

    others(
        lambda i: pl.semaphore_signal(
            barrier, inc=1, device_id=place(i), device_id_type=pl.DeviceIdType.MESH
        )
    )
    pl.semaphore_wait(barrier, n - 1)
    sources = (zero_ref, later)

    def copy(pair, k):
        where = place(k)
        to = (where[0] * n_tm + where[1]) * n_cores + where[2]
        return pltpu.make_async_remote_copy(
            src_ref=sources[pair].at[pl.ds(to * 2, 2)],
            dst_ref=got_ref.at[pair, me],
            send_sem=send_sem.at[pair, k],
            recv_sem=recv_sem.at[pair, k],
            device_id=where,
            device_id_type=pl.DeviceIdType.MESH,
        )

    def own(pair):
        return pltpu.make_async_copy(
            sources[pair].at[pl.ds(me * 2, 2)], got_ref.at[pair, me], local_sem.at[pair]
        )

    def send(pair):
        others(lambda i: copy(pair, i).start())
        own(pair).start()

    def finish(pair):
        own(pair).wait()
        others(lambda i: copy(pair, i).wait())

    send(0)
    loads = [
        pltpu.make_async_copy(zero_ref, later, load_sem.at[0]),
        pltpu.make_async_copy(blocks_ref.at[:, pl.ds(2 * FA, 2 * FA)], main_ref, load_sem.at[1]),
        pltpu.make_async_copy(halo_ref, next_ref, load_sem.at[2]),
    ]
    for load in loads:
        load.start()
    loads[0].wait()

    def widen(q, carry):
        turned[pl.ds(q * (FA + 1), FA), :] = later[q].astype(jnp.float32)
        return carry

    lax.fori_loop(0, FB // 2, widen, 0, unroll=2)
    stations = main_ref.shape[0]
    pick_tones(tone_ref, turned, picks, stations, True)

    def station(s, carry):
        rows = 2 * FA
        stream[0:rows, :] = main_ref[s].astype(jnp.float32)
        stream[rows : rows + FA, :] = next_ref[s].astype(jnp.float32)
        first_stage(s, delay_ref[s], valid_ref[s].astype(jnp.float32), one_ref, cos_ref, sin_ref,
                    stream, twist_re, twist_im)
        return carry

    loads[1].wait()
    loads[2].wait()
    lax.fori_loop(0, stations, station, 0)
    second_stage(two_ref, later, twist_re, twist_im, turned)
    send(1)
    pick_tones(tone_ref, turned, picks, stations, False)
    running = picks[...] + pltpu.roll(picks[...], 96, 1)
    flips = []
    for name, size in (("cores", n_cores), ("tm", n_tm)):
        bit = 1
        while bit < size:
            at = lax.axis_index(name)
            flips.append({name: at + bit * (1 - 2 * ((at // bit) % 2))})
            bit *= 2
    for r, partner in enumerate(flips):
        sent[r] = running
        passing = pltpu.make_async_remote_copy(
            src_ref=sent.at[r],
            dst_ref=arrived.at[r],
            send_sem=tone_send.at[r],
            recv_sem=tone_recv.at[r],
            device_id=partner,
            device_id_type=pl.DeviceIdType.MESH,
        )
        passing.start()
        passing.wait()
        running = running + arrived[r]
    tones_ref[...] = running * scale
    finish(0)
    finish(1)


def exchange(zero, blocks, halo, delays, valid, tone_chan, tables, sizes, scale):
    n = math.prod(sizes)
    rounds = (sizes[1] * sizes[2]).bit_length() - 1
    stations = blocks.shape[0]
    whole = lambda shape: pl.BlockSpec(shape, lambda i: (0,) * len(shape))
    smem = pl.BlockSpec(memory_space=pltpu.SMEM)
    return pl.pallas_call(
        lambda *refs: exchange_kernel(sizes, scale, *refs),
        out_shape=(
            jax.ShapeDtypeStruct((2, n, 2, FA, LANES), jnp.bfloat16),
            jax.ShapeDtypeStruct((NTONE, LANES), jnp.float32),
        ),
        grid=(1,),
        in_specs=[
            pl.BlockSpec(memory_space=pl.ANY),
            smem,
            smem,
            smem,
            pl.BlockSpec(memory_space=pl.ANY),
            pl.BlockSpec(memory_space=pl.ANY),
            whole((2 * FA, FA)),
            whole((FA, FB)),
            whole((FA, FB)),
            whole((FB // 2, 2 * FB)),
        ],
        out_specs=(pl.BlockSpec(memory_space=pl.ANY), whole((NTONE, LANES))),
        scratch_shapes=STAGE_SCRATCH
        + [
            pltpu.VMEM((FB // 2, FA, LANES), jnp.bfloat16),
            pltpu.VMEM((stations, 2 * FA, LANES), jnp.bfloat16),
            pltpu.VMEM((stations, FA, LANES), jnp.bfloat16),
            pltpu.VMEM((NTONE, LANES), jnp.float32),
            pltpu.VMEM((rounds, NTONE, LANES), jnp.float32),
            pltpu.VMEM((rounds, NTONE, LANES), jnp.float32),
            pltpu.SemaphoreType.DMA((2,)),
            pltpu.SemaphoreType.DMA((2, n)),
            pltpu.SemaphoreType.DMA((2, n)),
            pltpu.SemaphoreType.DMA((3,)),
            pltpu.SemaphoreType.DMA((rounds,)),
            pltpu.SemaphoreType.DMA((rounds,)),
        ],
        compiler_params=pltpu.CompilerParams(
            collective_id=0, has_side_effects=True, vmem_limit_bytes=VMEM_LIMIT
        ),
    )(zero, delays, valid, tone_chan, blocks, halo, *tables)


CB = 64


def correlate_kernel(scale, got_ref, out_ref, matrix, power, turned):
    lane = lax.broadcasted_iota(jnp.int32, (CB, LANES), 1)
    low = lane % 64 < 32
    n_time = got_ref.shape[2]
    rows = 4 * n_time
    pitch = rows + 1
    for u in range(2):
        for j in range(n_time):
            y0 = got_ref[u, 0, j].astype(jnp.float32)
            y1 = got_ref[u, 1, j].astype(jnp.float32)
            t = (u * n_time + j) * 2
            matrix[pl.ds(t, CB, stride=pitch), :] = jnp.where(low, y0, pltpu.roll(y1, 32, 1))
            matrix[pl.ds(t + 1, CB, stride=pitch), :] = jnp.where(low, pltpu.roll(y0, 96, 1), y1)
    left = lax.broadcasted_iota(jnp.int32, (S, LANES), 1) < 64
    left_half = lax.broadcasted_iota(jnp.int32, (S // 2, LANES), 1) < 64

    def channel(c, carry):
        values = matrix[pl.ds(c * pitch, rows), :].astype(jnp.bfloat16)
        gram = lax.dot_general(
            values, values, (((0,), (0,)), ((), ())), preferred_element_type=jnp.float32
        )
        upper = gram[:S] * scale
        lower = pltpu.roll(gram[S:] * scale, 64, 1)
        slot = pl.multiple_of((c % 16) * S, S)
        power[pl.ds(slot, S), :] = jnp.where(left, upper + lower, lower - upper)
        even = power[pl.ds(slot, S // 2, stride=2), :]
        odd = power[pl.ds(slot + 1, S // 2, stride=2), :]
        turned[pl.ds(c, S // 2, stride=CB + 1), :] = jnp.where(left_half, even, pltpu.roll(odd, 64, 1))
        turned[pl.ds(S // 2 * (CB + 1) + c, S // 2, stride=CB + 1), :] = jnp.where(
            left_half, pltpu.roll(even, 64, 1), odd
        )
        return carry

    lax.fori_loop(0, CB, channel, 0, unroll=16)
    for tile in range(S):
        at = tile * (CB + 1)
        out_ref[:, tile * LANES : (tile + 1) * LANES] = turned[at : at + CB, :]


def correlate(got, scale):
    _, n_stn, n_time, channels, _ = got.shape
    return pl.pallas_call(
        lambda *refs: correlate_kernel(scale, *refs),
        out_shape=jax.ShapeDtypeStruct((channels, 2 * S * S), jnp.float32),
        grid=(channels // CB,),
        in_specs=[pl.BlockSpec((2, n_stn, n_time, CB, LANES), lambda i: (0, 0, 0, i, 0))],
        out_specs=pl.BlockSpec((CB, 2 * S * S), lambda i: (i, 0)),
        scratch_shapes=[
            pltpu.VMEM((CB * (4 * n_time + 1), LANES), jnp.float32),
            pltpu.VMEM((16 * S, LANES), jnp.float32),
            pltpu.VMEM((S * (CB + 1), LANES), jnp.float32),
        ],
        compiler_params=pltpu.CompilerParams(vmem_limit_bytes=VMEM_LIMIT),
        cost_estimate=pl.CostEstimate(
            flops=2 * channels * 64 * 128 * 128, bytes_accessed=26 * 2**20, transcendentals=0
        ),
    )(got)


def fast_shards(samples, delays, valid, tone_chan):
    tables = fast_tables()
    sizes = tuple(lax.axis_size(name) for name in ("stn", "tm", "cores"))
    n_stn, n_tm, n_cores = sizes
    stations, stretch = samples.shape
    trailing = passed_along(samples[:, :MAXD], ("tm", "cores"), -1)
    blocks = samples.reshape(stations, stretch // LANES, LANES)
    zero = channelize_pair(0, blocks, (blocks, 2), delays, valid, tables)
    halo = trailing.reshape(stations, MAXD // LANES, LANES)
    channels = NCH // math.prod(sizes)
    scale = 1.0 / math.sqrt(stretch // (FA * FB) * n_tm * n_cores)
    got, picks = exchange(zero, blocks, halo, delays, valid, tone_chan, tables, sizes, scale)
    got = got.reshape(2, n_stn, n_tm * n_cores, channels, LANES)
    visibility = correlate(got, scale)
    mine = picks.reshape(NTONE, 2, 2, stations)[:, :, 0]
    phase_cal = jnp.transpose(mine, (2, 1, 0)).reshape(stations, 2 * NTONE)
    return (visibility, phase_cal)


def solution(mesh):
    sizes = mesh.shape
    body = fast_shards if sizes["stn"] == 2 and math.prod(sizes.values()) == 32 else shards
    return jax.shard_map(
        body,
        mesh=mesh,
        in_specs=(P("stn", ("tm", "cores")), P("stn"), P("stn"), P("stn", None)),
        out_specs=(P(("stn", "tm", "cores"), None), P("stn", None)),
        check_vma=False,
    )
```

```python
import math

import jax
import jax.numpy as jnp
import ml_dtypes
import numpy as np
from jax import lax
from jax.experimental import pallas as pl
from jax.experimental.pallas import tpu as pltpu
from jax.sharding import PartitionSpec as P

S = 64
NCH = 16384
FA = 256
FB = 128
NTONE = 64
MAXD = 32768


def passed_along(block, axis, distance):
    devices = range(lax.axis_size(axis))
    route = [(i - distance, i) for i in devices if i - distance in devices]
    return lax.ppermute(block, axis, route)


def make_tables():
    outer_idx = jnp.arange(FA, dtype=jnp.int32)
    phases = outer_idx[:, None] * outer_idx[None, :] % FA
    angles = 2.0 * math.pi / FA * phases.astype(jnp.float32)
    section_one = jnp.stack([jnp.cos(angles), -jnp.sin(angles)]).astype(jnp.bfloat16)
    inner_idx = jnp.arange(FB, dtype=jnp.int32)
    spectrum_len = FA * FB
    twist_idx = outer_idx[:, None] * inner_idx[None, :] % spectrum_len
    twists = 2.0 * math.pi / spectrum_len * twist_idx.astype(jnp.float32)
    norm_scale = 1.0 / math.sqrt(spectrum_len)
    twist_cos = jnp.cos(twists) * norm_scale
    twist_sin = jnp.sin(twists) * norm_scale
    half_idx = jnp.arange(FB // 2, dtype=jnp.int32)
    last_idx = inner_idx[:, None] * half_idx[None, :] % FB
    thetas = 2.0 * math.pi / FB * last_idx.astype(jnp.float32)
    cosine = jnp.cos(thetas)
    sine_val = jnp.sin(thetas)
    section_two = jnp.stack(
        [jnp.stack([cosine, -sine_val], axis=1), jnp.stack([sine_val, cosine], axis=1)]
    ).astype(jnp.bfloat16)
    return (section_one, twist_cos, twist_sin, section_two)


def channelize(window, usable, tables):
    section_one, twist_cos, twist_sin, section_two = tables
    spec_count = window.shape[0] // (FA * FB)
    blocks = window.reshape(spec_count, FA, FB)
    section_out = jnp.einsum(
        "xkn,bnm->bxkm", section_one, blocks, preferred_element_type=jnp.float32
    )
    real_part = section_out[:, 0] * twist_cos + section_out[:, 1] * twist_sin
    imag_part = section_out[:, 1] * twist_cos - section_out[:, 0] * twist_sin
    twisted = jnp.stack([real_part, imag_part], axis=1).astype(jnp.bfloat16)
    product = jnp.einsum(
        "xnrq,bxkn->brqk", section_two, twisted, preferred_element_type=jnp.float32
    )
    return (product.reshape(spec_count, 2, NCH) * usable).astype(jnp.bfloat16)


def cross_power(matrix):
    gram = jnp.einsum("cta,ctb->cab", matrix, matrix, preferred_element_type=jnp.float32)
    real_re = gram[:, :S, :S]
    imag_im = gram[:, S:, S:]
    imag_re = gram[:, S:, :S]
    real_im = gram[:, :S, S:]
    channels = gram.shape[0]
    first = (real_re + imag_im).reshape(channels, S * S)
    second = (imag_re - real_im).reshape(channels, S * S)
    return jnp.concatenate([first, second], axis=1)


def shards(samples, delays, valid, tone_chan):
    tables = make_tables()
    stretch = samples.shape[1]
    spectrum_len = FA * FB
    trailing = passed_along(samples[:, :MAXD], ("tm", "cores"), -1)
    extended = jnp.concatenate([samples, trailing], axis=1)
    chan_ids = jnp.arange(NCH, dtype=jnp.int32)

    def station(inputs):
        stream, shift_by, usable, tone_ids = inputs
        window = lax.dynamic_slice_in_dim(stream, shift_by, stretch)
        spectra = channelize(window, usable.astype(jnp.float32), tables)
        totals = jnp.sum(spectra, axis=0, dtype=jnp.float32)
        selector = (chan_ids[:, None] == tone_ids[None, :]).astype(jnp.float32)
        picked = jnp.dot(
            totals, selector, precision=lax.Precision.HIGHEST, preferred_element_type=jnp.float32
        )
        return (spectra, picked.reshape(2 * NTONE))

    spectra, tone_picks = lax.map(station, (extended, delays, valid, tone_chan))
    spectra_all = stretch // spectrum_len * lax.axis_size("tm") * lax.axis_size("cores")
    norm_scale = 1.0 / math.sqrt(spectra_all)
    phase_cal = lax.psum(tone_picks, ("tm", "cores")) * norm_scale
    local_stn = spectra.shape[0]
    spec_here = spectra.shape[1]
    n_stn = lax.axis_size("stn")
    n_tm = lax.axis_size("tm")
    received = lax.all_to_all(spectra[None], ("stn", "tm"), split_axis=4, concat_axis=0, tiled=True)
    block_in = received.shape[4]
    arranged = received.reshape(n_stn, n_tm, local_stn, spec_here, 2, block_in)
    turned = jnp.transpose(arranged, (0, 2, 1, 3, 4, 5)).reshape(
        n_stn * local_stn, n_tm * spec_here, 2, block_in
    )
    block = turned.shape[3]
    halves = turned.reshape(turned.shape[0], turned.shape[1], 2, 2, block // 2)
    halves = lax.all_to_all(halves, "cores", split_axis=3, concat_axis=1, tiled=True)
    turned = halves.reshape(halves.shape[0], halves.shape[1], 2, block // 2)
    rows = turned.shape[1]
    matrix = jnp.transpose(turned, (3, 1, 2, 0)).reshape(turned.shape[3], rows, 2 * S)
    partial_value = cross_power(matrix)
    return (partial_value * norm_scale, phase_cal)


LANES = 128
VMEM_LIMIT = 56 * 1024 * 1024


def fast_tables():
    def turn(left, right, period):
        angle = np.float32(2.0 * math.pi / period)
        phases = (np.arange(left)[:, None] * np.arange(right)[None, :] % period).astype(np.float32)
        return np.cos(angle * phases), np.sin(angle * phases)

    cosine, sine = turn(FA, FA, FA)
    first = np.concatenate([cosine, -sine], axis=0).astype(ml_dtypes.bfloat16)
    cosine, sine = turn(FA, FB, FA * FB)
    norm_scale = np.float32(1.0 / math.sqrt(FA * FB))
    twist_cos, twist_sin = cosine * norm_scale, sine * norm_scale
    cosine, sine = turn(FB // 2, FB, FB)
    last = np.concatenate([cosine, sine], axis=1).astype(ml_dtypes.bfloat16)
    return tuple(jnp.asarray(table) for table in (first, twist_cos, twist_sin, last))


def first_stage(s, delay, usable, one_ref, cos_ref, sin_ref, stream, twist_re, twist_im):
    rows = 2 * FA
    whole = delay // LANES
    part = delay % LANES
    lane = lax.broadcasted_iota(jnp.int32, (rows, LANES), 1)
    here = stream[pl.ds(whole, rows), :]
    after = stream[pl.ds(whole + 1, rows), :]
    mixed = jnp.where(lane < part, after, here)
    shifted = pltpu.roll(mixed, (LANES - part) % LANES, 1).astype(jnp.bfloat16)
    both = jnp.concatenate([shifted[:FA], shifted[FA:]], axis=1)
    section = jnp.dot(one_ref[...], both, preferred_element_type=jnp.float32)
    cosine = cos_ref[...] * usable
    sine = sin_ref[...] * usable
    for t in range(2):
        re = section[:FA, t * LANES : (t + 1) * LANES]
        im = section[FA:, t * LANES : (t + 1) * LANES]
        twist_re[pl.ds(t * 32 + s, FA, stride=PITCH), :] = re * cosine + im * sine
        twist_im[pl.ds(t * 32 + s, FA, stride=PITCH), :] = im * cosine - re * sine


def second_stage(two_ref, out_ref, twist_re, twist_im, turned):
    def second(k, carry):
        re = twist_re[pl.ds(k * PITCH, 64), :].astype(jnp.bfloat16)
        im = twist_im[pl.ds(k * PITCH, 64), :].astype(jnp.bfloat16)
        right = jnp.concatenate(
            [jnp.concatenate([re, im], axis=1), jnp.concatenate([im, -re], axis=1)], axis=0
        )
        product = lax.dot_general(
            two_ref[...], right, (((1,), (1,)), ((), ())), preferred_element_type=jnp.float32
        )
        turned[pl.ds(k, FB // 2, stride=FA + 1), :] = product
        return carry

    lax.fori_loop(0, FA, second, 0, unroll=16)

    def write(q, carry):
        out_ref[q] = turned[pl.ds(q * (FA + 1), FA), :].astype(jnp.bfloat16)
        return carry

    lax.fori_loop(0, FB // 2, write, 0, unroll=2)


PITCH = 65
TOGETHER = 4
STAGE_SCRATCH = [
    pltpu.VMEM((3 * FA + 8, LANES), jnp.float32),
    pltpu.VMEM((FA * PITCH + 7, LANES), jnp.float32),
    pltpu.VMEM((FA * PITCH + 7, LANES), jnp.float32),
    pltpu.VMEM(((FA + 1) * FB // 2, LANES), jnp.float32),
]


def channelize_kernel(delay_ref, valid_ref, main_ref, next_ref, one_ref, cos_ref, sin_ref, two_ref,
                      out_ref, stream, twist_re, twist_im, turned):
    rows = 2 * FA
    for i in range(TOGETHER):
        stream[i, 0:rows, :] = main_ref[i].astype(jnp.float32)
        stream[i, rows : rows + FA, :] = next_ref[i].astype(jnp.float32)
    for i in range(TOGETHER):
        s = pl.program_id(0) * TOGETHER + i
        first_stage(s, delay_ref[s], valid_ref[s].astype(jnp.float32), one_ref, cos_ref, sin_ref,
                    stream.at[i], twist_re, twist_im)

    @pl.when(pl.program_id(0) == pl.num_programs(0) - 1)
    def _():
        second_stage(two_ref, out_ref, twist_re, twist_im, turned)


def channelize_pair(pair, blocks, following, delays, valid, tables):
    first, twist_cos, twist_sin, last = tables
    source, next_at = following
    whole = lambda shape: pl.BlockSpec(shape, lambda s, *_: (0,) * len(shape))
    return pl.pallas_call(
        channelize_kernel,
        out_shape=jax.ShapeDtypeStruct((FB // 2, FA, LANES), jnp.bfloat16),
        grid_spec=pltpu.PrefetchScalarGridSpec(
            num_scalar_prefetch=2,
            grid=(blocks.shape[0] // TOGETHER,),
            in_specs=[
                pl.BlockSpec((TOGETHER, 2 * FA, LANES), lambda s, *_: (s, pair, 0)),
                pl.BlockSpec((TOGETHER, FA, LANES), lambda s, *_: (s, next_at, 0)),
                whole((2 * FA, FA)),
                whole((FA, FB)),
                whole((FA, FB)),
                whole((FB // 2, 2 * FB)),
            ],
            out_specs=whole((FB // 2, FA, LANES)),
            scratch_shapes=[pltpu.VMEM((TOGETHER, 3 * FA + 8, LANES), jnp.float32)] + STAGE_SCRATCH[1:],
        ),
        compiler_params=pltpu.CompilerParams(vmem_limit_bytes=VMEM_LIMIT),
        cost_estimate=pl.CostEstimate(
            flops=3 * 2 * 64 * 256 * 256 * 256, bytes_accessed=10 * 2**20, transcendentals=0
        ),
    )(delays, valid, blocks, source, first, twist_cos, twist_sin, last)


def linear_index(sizes):
    n_stn, n_tm, n_cores = sizes
    return (lax.axis_index("stn") * n_tm + lax.axis_index("tm")) * n_cores + lax.axis_index("cores")


def pick_tones(tone_ref, turned, picks, stations, first):
    lane = lax.broadcasted_iota(jnp.int32, (1, LANES), 1) % 32

    def tone(k, carry):
        row = jnp.zeros((1, LANES), jnp.float32)
        for s in range(stations):
            channel = tone_ref[s, k]
            row = jnp.where(lane == s, turned[pl.ds(channel + channel // FA, 1), :], row)
        row = row.astype(jnp.bfloat16).astype(jnp.float32)
        picks[pl.ds(k, 1), :] = row if first else picks[pl.ds(k, 1), :] + row
        return carry

    lax.fori_loop(0, NTONE, tone, 0)


def exchange_kernel(sizes, scale, zero_ref, delay_ref, valid_ref, tone_ref, blocks_ref, halo_ref, one_ref,
                    cos_ref, sin_ref, two_ref, got_ref, tones_ref, stream, twist_re, twist_im,
                    turned, later, main_ref, next_ref, picks, sent, arrived, local_sem, send_sem, recv_sem, load_sem,
                    tone_send, tone_recv):
    _, n_tm, n_cores = sizes
    n = math.prod(sizes)
    me = linear_index(sizes)

    self_at = 4

    def place(i):
        turn = (i + i // n_tm) % 4
        return (
            (lax.axis_index("stn") + turn // 2) % 2,
            (lax.axis_index("tm") + 3 * i + 4) % n_tm,
            (lax.axis_index("cores") + turn) % 2,
        )

    def others(body):
        def step(i, carry):
            body(i)
            return carry

        lax.fori_loop(0, self_at, step, 0)
        lax.fori_loop(self_at + 1, n, step, 0)

    barrier = pltpu.get_barrier_semaphore()

    others(
        lambda i: pl.semaphore_signal(
            barrier, inc=1, device_id=place(i), device_id_type=pl.DeviceIdType.MESH
        )
    )
    pl.semaphore_wait(barrier, n - 1)
    sources = (zero_ref, later)

    def copy(pair, k):
        where = place(k)
        to = (where[0] * n_tm + where[1]) * n_cores + where[2]
        return pltpu.make_async_remote_copy(
            src_ref=sources[pair].at[pl.ds(to * 2, 2)],
            dst_ref=got_ref.at[pair, me],
            send_sem=send_sem.at[pair, k],
            recv_sem=recv_sem.at[pair, k],
            device_id=where,
            device_id_type=pl.DeviceIdType.MESH,
        )

    def own(pair):
        return pltpu.make_async_copy(
            sources[pair].at[pl.ds(me * 2, 2)], got_ref.at[pair, me], local_sem.at[pair]
        )

    def send(pair):
        others(lambda i: copy(pair, i).start())
        own(pair).start()

    def finish(pair):
        own(pair).wait()
        others(lambda i: copy(pair, i).wait())

    send(0)
    loads = [
        pltpu.make_async_copy(zero_ref, later, load_sem.at[0]),
        pltpu.make_async_copy(blocks_ref.at[:, pl.ds(2 * FA, 2 * FA)], main_ref, load_sem.at[1]),
        pltpu.make_async_copy(halo_ref, next_ref, load_sem.at[2]),
    ]
    for load in loads:
        load.start()
    loads[0].wait()

    def widen(q, carry):
        turned[pl.ds(q * (FA + 1), FA), :] = later[q].astype(jnp.float32)
        return carry

    lax.fori_loop(0, FB // 2, widen, 0, unroll=2)
    stations = main_ref.shape[0]
    pick_tones(tone_ref, turned, picks, stations, True)

    def station(s, carry):
        rows = 2 * FA
        stream[0:rows, :] = main_ref[s].astype(jnp.float32)
        stream[rows : rows + FA, :] = next_ref[s].astype(jnp.float32)
        first_stage(s, delay_ref[s], valid_ref[s].astype(jnp.float32), one_ref, cos_ref, sin_ref,
                    stream, twist_re, twist_im)
        return carry

    loads[1].wait()
    loads[2].wait()
    lax.fori_loop(0, stations, station, 0)
    second_stage(two_ref, later, twist_re, twist_im, turned)
    send(1)
    pick_tones(tone_ref, turned, picks, stations, False)
    running = picks[...] + pltpu.roll(picks[...], 96, 1)
    flips = []
    for name, size in (("cores", n_cores), ("tm", n_tm)):
        bit = 1
        while bit < size:
            at = lax.axis_index(name)
            flips.append({name: at + bit * (1 - 2 * ((at // bit) % 2))})
            bit *= 2
    for r, partner in enumerate(flips):
        sent[r] = running
        passing = pltpu.make_async_remote_copy(
            src_ref=sent.at[r],
            dst_ref=arrived.at[r],
            send_sem=tone_send.at[r],
            recv_sem=tone_recv.at[r],
            device_id=partner,
            device_id_type=pl.DeviceIdType.MESH,
        )
        passing.start()
        passing.wait()
        running = running + arrived[r]
    tones_ref[...] = running * scale
    finish(0)
    finish(1)


def exchange(zero, blocks, halo, delays, valid, tone_chan, tables, sizes, scale):
    n = math.prod(sizes)
    rounds = (sizes[1] * sizes[2]).bit_length() - 1
    stations = blocks.shape[0]
    whole = lambda shape: pl.BlockSpec(shape, lambda i: (0,) * len(shape))
    smem = pl.BlockSpec(memory_space=pltpu.SMEM)
    return pl.pallas_call(
        lambda *refs: exchange_kernel(sizes, scale, *refs),
        out_shape=(
            jax.ShapeDtypeStruct((2, n, 2, FA, LANES), jnp.bfloat16),
            jax.ShapeDtypeStruct((NTONE, LANES), jnp.float32),
        ),
        grid=(1,),
        in_specs=[
            pl.BlockSpec(memory_space=pl.ANY),
            smem,
            smem,
            smem,
            pl.BlockSpec(memory_space=pl.ANY),
            pl.BlockSpec(memory_space=pl.ANY),
            whole((2 * FA, FA)),
            whole((FA, FB)),
            whole((FA, FB)),
            whole((FB // 2, 2 * FB)),
        ],
        out_specs=(pl.BlockSpec(memory_space=pl.ANY), whole((NTONE, LANES))),
        scratch_shapes=STAGE_SCRATCH
        + [
            pltpu.VMEM((FB // 2, FA, LANES), jnp.bfloat16),
            pltpu.VMEM((stations, 2 * FA, LANES), jnp.bfloat16),
            pltpu.VMEM((stations, FA, LANES), jnp.bfloat16),
            pltpu.VMEM((NTONE, LANES), jnp.float32),
            pltpu.VMEM((rounds, NTONE, LANES), jnp.float32),
            pltpu.VMEM((rounds, NTONE, LANES), jnp.float32),
            pltpu.SemaphoreType.DMA((2,)),
            pltpu.SemaphoreType.DMA((2, n)),
            pltpu.SemaphoreType.DMA((2, n)),
            pltpu.SemaphoreType.DMA((3,)),
            pltpu.SemaphoreType.DMA((rounds,)),
            pltpu.SemaphoreType.DMA((rounds,)),
        ],
        compiler_params=pltpu.CompilerParams(
            collective_id=0, has_side_effects=True, vmem_limit_bytes=VMEM_LIMIT
        ),
    )(zero, delays, valid, tone_chan, blocks, halo, *tables)


CB = 64


def correlate_kernel(scale, got_ref, out_ref, matrix, power, turned):
    lane = lax.broadcasted_iota(jnp.int32, (CB, LANES), 1)
    low = lane % 64 < 32
    n_time = got_ref.shape[2]
    rows = 4 * n_time
    pitch = rows + 1
    for u in range(2):
        for j in range(n_time):
            y0 = got_ref[u, 0, j].astype(jnp.float32)
            y1 = got_ref[u, 1, j].astype(jnp.float32)
            t = (u * n_time + j) * 2
            matrix[pl.ds(t, CB, stride=pitch), :] = jnp.where(low, y0, pltpu.roll(y1, 32, 1))
            matrix[pl.ds(t + 1, CB, stride=pitch), :] = jnp.where(low, pltpu.roll(y0, 96, 1), y1)
    left = lax.broadcasted_iota(jnp.int32, (S, LANES), 1) < 64
    left_half = lax.broadcasted_iota(jnp.int32, (S // 2, LANES), 1) < 64

    def channel(c, carry):
        values = matrix[pl.ds(c * pitch, rows), :].astype(jnp.bfloat16)
        gram = lax.dot_general(
            values, values, (((0,), (0,)), ((), ())), preferred_element_type=jnp.float32
        )
        upper = gram[:S] * scale
        lower = pltpu.roll(gram[S:] * scale, 64, 1)
        slot = pl.multiple_of((c % 16) * S, S)
        power[pl.ds(slot, S), :] = jnp.where(left, upper + lower, lower - upper)
        even = power[pl.ds(slot, S // 2, stride=2), :]
        odd = power[pl.ds(slot + 1, S // 2, stride=2), :]
        turned[pl.ds(c, S // 2, stride=CB + 1), :] = jnp.where(left_half, even, pltpu.roll(odd, 64, 1))
        turned[pl.ds(S // 2 * (CB + 1) + c, S // 2, stride=CB + 1), :] = jnp.where(
            left_half, pltpu.roll(even, 64, 1), odd
        )
        return carry

    lax.fori_loop(0, CB, channel, 0, unroll=4)
    for tile in range(S):
        at = tile * (CB + 1)
        out_ref[:, tile * LANES : (tile + 1) * LANES] = turned[at : at + CB, :]


def correlate(got, scale):
    _, n_stn, n_time, channels, _ = got.shape
    return pl.pallas_call(
        lambda *refs: correlate_kernel(scale, *refs),
        out_shape=jax.ShapeDtypeStruct((channels, 2 * S * S), jnp.float32),
        grid=(channels // CB,),
        in_specs=[pl.BlockSpec((2, n_stn, n_time, CB, LANES), lambda i: (0, 0, 0, i, 0))],
        out_specs=pl.BlockSpec((CB, 2 * S * S), lambda i: (i, 0)),
        scratch_shapes=[
            pltpu.VMEM((CB * (4 * n_time + 1), LANES), jnp.float32),
            pltpu.VMEM((16 * S, LANES), jnp.float32),
            pltpu.VMEM((S * (CB + 1), LANES), jnp.float32),
        ],
        compiler_params=pltpu.CompilerParams(vmem_limit_bytes=VMEM_LIMIT),
        cost_estimate=pl.CostEstimate(
            flops=2 * channels * 64 * 128 * 128, bytes_accessed=26 * 2**20, transcendentals=0
        ),
    )(got)


def fast_shards(samples, delays, valid, tone_chan):
    tables = fast_tables()
    sizes = tuple(lax.axis_size(name) for name in ("stn", "tm", "cores"))
    n_stn, n_tm, n_cores = sizes
    stations, stretch = samples.shape
    trailing = passed_along(samples[:, :MAXD], ("tm", "cores"), -1)
    blocks = samples.reshape(stations, stretch // LANES, LANES)
    zero = channelize_pair(0, blocks, (blocks, 2), delays, valid, tables)
    halo = trailing.reshape(stations, MAXD // LANES, LANES)
    channels = NCH // math.prod(sizes)
    scale = 1.0 / math.sqrt(stretch // (FA * FB) * n_tm * n_cores)
    got, picks = exchange(zero, blocks, halo, delays, valid, tone_chan, tables, sizes, scale)
    got = got.reshape(2, n_stn, n_tm * n_cores, channels, LANES)
    visibility = correlate(got, scale)
    mine = picks.reshape(NTONE, 2, 2, stations)[:, :, 0]
    phase_cal = jnp.transpose(mine, (2, 1, 0)).reshape(stations, 2 * NTONE)
    return (visibility, phase_cal)


def solution(mesh):
    sizes = mesh.shape
    body = fast_shards if sizes["stn"] == 2 and math.prod(sizes.values()) == 32 else shards
    return jax.shard_map(
        body,
        mesh=mesh,
        in_specs=(P("stn", ("tm", "cores")), P("stn"), P("stn"), P("stn", None)),
        out_specs=(P(("stn", "tm", "cores"), None), P("stn", None)),
        check_vma=False,
    )
```
